512 devices in a mesh: row: 32 (over y_hi, x, core), col: 16 (over y_lo, z).
Axes of the slice: x: 4, y: 8 (y_hi: 4, y_lo: 2; y = y_hi * 2 + y_lo), z: 8, core: 2. Of those that a mesh axis runs over, the one named last changes fastest.
Arguments:
- node_inputs: bfloat16 [65536, 128], P(('col', 'row')), may hold values from -6 to 6
- weight: bfloat16 [128, 256], replicated, may hold values from -0.5 to 0.5
- bias: float32 [256], replicated, may hold values from -2 to 2
- edge_tiles: bfloat16 [32, 1408, 128, 128], P('row', 'col'), may hold values from 0 to 1, as said below
- block_coords: int32 [32, 1408, 2], P('row', 'col'), may hold values from 0 to 31, as said below
- block_counts: int32 [32, 16], P('row', 'col'), may hold values from 1 to 88, as said below
- out_cotangent: bfloat16 [65536, 256], P(('row', 'col')), may hold values from -6 to 6
Outputs:
- activations: bfloat16 [65536, 256], P(('row', 'col'))
- grad_inputs: bfloat16 [65536, 128], P(('col', 'row'))
- grad_weight: float32 [128, 256], replicated
- grad_bias: float32 [256], replicated
The draws below stay inside these ranges and needn't reach their ends.
Inputs may be any that keep to these rules, and one draw needn't show every extreme that they name: `edge_tiles`: each entry is 0 or 1. `block_coords`: within one grid position the 88 slots name distinct blocks; entry 0 is a block row below 16, entry 1 a block column below 32. Slots at or after the position's count are not part of A. `block_counts`: some grid position has all 88 slots live.
All inputs are finite; a program needn't handle non-finite values.
Results may differ from the reference program's by a relative error of at most 0.025.
Values may be sent and summed in bfloat16 or wider, within the bound.
No kernel may reach another device: no remote copies, remote signals or barrier semaphores. Data moves between devices by JAX's collectives and lax.ppermute only.
A program may use at most 64 MiB of HBM per device.

```python
import jax
import jax.numpy as jnp
from jax import lax

F_IN = 128
F_HID = 256
BLOCK = 128
ROWS_DEV = 2048
COLS_DEV = 4096
NODES = 65536
MAXB = 88
N_ROW = 32
N_COL = 16


def draw_node_inputs(key, part):
    key = jax.random.fold_in(key, 21)
    offsets = jax.random.uniform(jax.random.fold_in(key, 1), (1, F_IN), jnp.float32, -1.5, 1.5)
    noise_key = jax.random.fold_in(key, 2)
    noise = jnp.clip(jax.random.normal(noise_key, (NODES, F_IN), jnp.float32), -4.0, 4.0)
    return (offsets + noise).astype(jnp.bfloat16)


def draw_edge_tiles(key, part):
    levels = jax.random.randint(jax.random.fold_in(key, 14), (N_ROW, N_COL * MAXB, BLOCK, BLOCK), 0, 8)
    return (levels == 0).astype(jnp.bfloat16)


def draw_block_coords(key, part):
    row_blocks = ROWS_DEV // BLOCK
    col_blocks = COLS_DEV // BLOCK
    keys = jax.random.split(jax.random.fold_in(key, 11), N_ROW * N_COL)

    def pick_blocks(sub_key):
        return jax.random.permutation(sub_key, row_blocks * col_blocks)[:MAXB]
    chosen = jax.vmap(pick_blocks)(keys).astype(jnp.int32)
    coords = jnp.stack([chosen // col_blocks, chosen % col_blocks], axis=-1)
    return coords.reshape(N_ROW, N_COL * MAXB, 2).astype(jnp.int32)


def draw_block_counts(key, part):
    shifts = jax.random.randint(jax.random.fold_in(key, 12), (N_ROW * N_COL,), 0, 4)
    fulls = jnp.full((N_ROW * N_COL,), MAXB, jnp.int32)
    counts = jnp.maximum(jnp.right_shift(fulls, shifts), 1)
    busiest = jax.random.randint(jax.random.fold_in(key, 13), (), 0, N_ROW * N_COL)
    counts = jnp.where(jnp.arange(N_ROW * N_COL, dtype=jnp.int32) == busiest, MAXB, counts)
    return counts.reshape(N_ROW, N_COL).astype(jnp.int32)


def level_of(stream_key, dims, pieces, smallest, top_value):
    loudness = 1.0
    for position, blocks in pieces:
        draws = jax.random.uniform(jax.random.fold_in(jax.random.fold_in(stream_key, 6), position), (blocks,), jnp.float32, smallest / len(pieces), top_value / len(pieces))
        loudness = loudness * jnp.repeat(jnp.exp(draws), dims[position] // blocks).reshape((-1,) + (1,) * (len(dims) - 1 - position))
    return loudness


def scatter_about(own_key, shape, deviation, bound, shards=(), kind=jnp.bfloat16):
    level = level_of(own_key, shape, shards, -0.22, 0.18) if shards else 1.0
    result = jax.random.normal(own_key, shape, jnp.float32) * deviation * level
    return jnp.minimum(jnp.maximum(result, -bound), bound).astype(kind)


def setup_inputs(seed: int = 0) -> dict:
    arg_keys = jax.random.split(jax.random.key(seed), 8)
    node_inputs = draw_node_inputs(jax.random.fold_in(arg_keys[7], 71), 0)
    weight = scatter_about(arg_keys[1], (F_IN, F_HID), F_IN ** -0.5, 0.5)
    bias = scatter_about(arg_keys[2], (F_HID,), 0.5, 2.0, (), jnp.float32)
    edge_tiles = draw_edge_tiles(jax.random.fold_in(arg_keys[7], 71), 0)
    block_coords = draw_block_coords(jax.random.fold_in(arg_keys[7], 71), 0)
    block_counts = draw_block_counts(jax.random.fold_in(arg_keys[7], 71), 0)
    out_cotangent = scatter_about(arg_keys[6], (NODES, F_HID), 1.0, 6.0, ((0, 512),))
    return dict(node_inputs=node_inputs, weight=weight, bias=bias, edge_tiles=edge_tiles, block_coords=block_coords, block_counts=block_counts, out_cotangent=out_cotangent)


def spread_piece(tile_stack, slot_coords, live_mask, features, block_total, transpose):
    block_size = tile_stack.shape[1]
    width = features.shape[1]
    feature_blocks = features.reshape(-1, block_size, width).astype(jnp.float32)
    tiles_live = tile_stack.astype(jnp.float32) * live_mask[:, None, None]
    if transpose:
        selected = jnp.take(feature_blocks, slot_coords[:, 0], axis=0)
        product = jnp.einsum('sab,saf->sbf', tiles_live, selected)
        target = slot_coords[:, 1]
    else:
        selected = jnp.take(feature_blocks, slot_coords[:, 1], axis=0)
        product = jnp.einsum('sab,sbf->saf', tiles_live, selected)
        target = slot_coords[:, 0]
    summed = jax.ops.segment_sum(product, target, num_segments=block_total)
    return summed.reshape(block_total * block_size, width)

def reference(node_inputs, weight, bias, edge_tiles, block_coords, block_counts, out_cotangent):
    row_ratio = N_ROW // N_COL
    row_blocks = ROWS_DEV // BLOCK
    col_blocks = COLS_DEV // BLOCK
    tiles_grid = edge_tiles.reshape(N_ROW, N_COL, MAXB, BLOCK, BLOCK)
    coords_grid = block_coords.reshape(N_ROW, N_COL, MAXB, 2)
    slot_ids = jnp.arange(MAXB, dtype=jnp.int32)
    live_grid = (slot_ids[None, None, :] < block_counts[:, :, None]).astype(jnp.float32)

    def degree_row(row_index):
        tiles_row = tiles_grid[row_index]
        coords_row = coords_grid[row_index]
        live_row = live_grid[row_index]
        row_counts = lax.optimization_barrier(jnp.sum(tiles_row, axis=3, dtype=jnp.float32)) * live_row[..., None]
        col_counts = lax.optimization_barrier(jnp.sum(tiles_row, axis=2, dtype=jnp.float32)) * live_row[..., None]

        def row_segments(values, targets):
            return jax.ops.segment_sum(values, targets, num_segments=row_blocks)

        def col_segments(values, targets):
            return jax.ops.segment_sum(values, targets, num_segments=col_blocks)
        row_part = jax.vmap(row_segments)(row_counts, coords_row[..., 0])
        col_part = jax.vmap(col_segments)(col_counts, coords_row[..., 1])
        return (lax.optimization_barrier(jnp.sum(row_part, axis=0)).reshape(ROWS_DEV), col_part.reshape(N_COL, COLS_DEV))
    row_count_grid, col_count_grid = lax.map(degree_row, jnp.arange(N_ROW, dtype=jnp.int32))
    row_degree = 1.0 + row_count_grid.reshape(NODES)
    col_degree = 1.0 + lax.optimization_barrier(jnp.sum(col_count_grid, axis=0)).reshape(NODES)
    row_scale = lax.rsqrt(row_degree)[:, None]
    col_scale = lax.rsqrt(col_degree)[:, None]
    hidden = (jnp.dot(node_inputs, weight, preferred_element_type=jnp.float32) * col_scale).astype(jnp.bfloat16)
    hidden_pieces = hidden.reshape(N_COL, COLS_DEV, F_HID)

    def forward_row(row_index):

        def add_piece(running, col_index):
            features = hidden_pieces[col_index]
            partial_value = spread_piece(tiles_grid[row_index, col_index], coords_grid[row_index, col_index], live_grid[row_index, col_index], features, row_blocks, False)
            start = (row_index % row_ratio * ROWS_DEV).astype(jnp.int32)
            own_rows = lax.dynamic_slice_in_dim(features, start, ROWS_DEV, 0).astype(jnp.float32)
            partial_value = partial_value + jnp.where(col_index == row_index // row_ratio, own_rows, jnp.zeros_like(own_rows))
            rounded = lax.optimization_barrier(partial_value.astype(jnp.bfloat16))
            return (running + rounded.astype(jnp.float32), None)
        running, unused = lax.scan(add_piece, jnp.zeros((ROWS_DEV, F_HID), jnp.float32), jnp.arange(N_COL, dtype=jnp.int32))
        return running
    summed = lax.map(forward_row, jnp.arange(N_ROW, dtype=jnp.int32)).reshape(NODES, F_HID)
    preactivation = row_scale * summed + bias
    sigmoid_values = jax.nn.sigmoid(preactivation)
    activations = (preactivation * sigmoid_values).astype(jnp.bfloat16)
    grad_pre = out_cotangent.astype(jnp.float32) * sigmoid_values * (1.0 + preactivation * (1.0 - sigmoid_values))
    grad_bias = lax.optimization_barrier(jnp.sum(grad_pre, axis=0))
    cotangent = (row_scale * grad_pre).astype(jnp.bfloat16)
    cotangent_pieces = cotangent.reshape(N_ROW, ROWS_DEV, F_HID)

    def backward_col(col_index):

        def add_piece(running, row_index):
            cotangent_rows = cotangent_pieces[row_index]
            partial_value = spread_piece(tiles_grid[row_index, col_index], coords_grid[row_index, col_index], live_grid[row_index, col_index], cotangent_rows, col_blocks, True)
            start = (row_index % row_ratio * ROWS_DEV).astype(jnp.int32)
            self_term = lax.dynamic_update_slice_in_dim(jnp.zeros((COLS_DEV, F_HID), jnp.float32), cotangent_rows.astype(jnp.float32), start, 0)
            partial_value = partial_value + jnp.where(col_index == row_index // row_ratio, self_term, jnp.zeros_like(self_term))
            rounded = lax.optimization_barrier(partial_value.astype(jnp.bfloat16))
            return (running + rounded.astype(jnp.float32), None)
        running, unused = lax.scan(add_piece, jnp.zeros((COLS_DEV, F_HID), jnp.float32), jnp.arange(N_ROW, dtype=jnp.int32))
        return running
    summed_back = lax.map(backward_col, jnp.arange(N_COL, dtype=jnp.int32)).reshape(NODES, F_HID)
    grad_hidden = (col_scale * summed_back).astype(jnp.bfloat16)
    grad_weight = jnp.dot(node_inputs.T, grad_hidden, preferred_element_type=jnp.float32)
    grad_inputs = jnp.dot(grad_hidden, weight.T, preferred_element_type=jnp.float32).astype(jnp.bfloat16)
    return (activations, grad_inputs, grad_weight, grad_bias)
```

```python
import jax
import jax.numpy as jnp
from jax import lax
from jax.experimental import pallas as pl
from jax.experimental.pallas import tpu as pltpu
from jax.sharding import PartitionSpec as P


BLK = 128
GROUP = 4
F32 = jnp.float32
BF16 = jnp.bfloat16
VMEM = pl.BlockSpec(memory_space=pltpu.VMEM)
SMEM = pl.BlockSpec(memory_space=pltpu.SMEM)
NT = (((1,), (1,)), ((), ()))
TN = (((0,), (0,)), ((), ()))


def call(kernel, name, operands, specs, outs, scratch=(), flops=0, limit=32):
    single = not isinstance(outs, (list, tuple))
    moved = sum(x.size * x.dtype.itemsize for x in operands)
    moved += sum(
        o.dtype.itemsize * _size(o.shape) for o in ([outs] if single else outs)
    )
    return pl.pallas_call(
        kernel,
        out_shape=outs,
        in_specs=specs,
        out_specs=VMEM if single else [VMEM] * len(outs),
        scratch_shapes=list(scratch),
        compiler_params=pltpu.CompilerParams(vmem_limit_bytes=limit << 20),
        cost_estimate=pl.CostEstimate(flops=flops, bytes_accessed=moved, transcendentals=0),
        name=name,
    )(*operands)


def _size(shape):
    total = 1
    for n in shape:
        total *= n
    return total


def struct(shape, dtype):
    return jax.ShapeDtypeStruct(shape, dtype)


def split(value):
    high = value.astype(BF16).astype(F32)
    return high, value - high


def slot_of(q, parity, half):
    return ((q & 1) ^ parity) * half + (q >> 1)


def eye(n):
    return lax.broadcasted_iota(jnp.int32, (n, n), 0) == lax.broadcasted_iota(jnp.int32, (n, n), 1)


def count_kernel(info, coords, tiles, own, other, rows, col_acc, row_acc):
    half = own.shape[0]
    col_acc[...] = jnp.zeros_like(col_acc)
    row_acc[...] = jnp.zeros_like(row_acc)
    count, parity = info[0], info[1]
    ones = jnp.ones((8, BLK), BF16)

    def group(g, carry):
        for u in range(GROUP):
            s = g * GROUP + u
            live = jnp.where(s < count, 1.0, 0.0).astype(F32)
            tile = tiles[s]
            column = jnp.sum(tile.reshape(BLK // 16, 16, BLK), axis=0)
            line = lax.dot_general(ones, tile, NT, preferred_element_type=F32)
            at = slot_of(coords[s, 1], parity, half)
            col_acc[at] += column.astype(F32) * live
            row_acc[coords[s, 0]] += line * live
        return carry

    lax.fori_loop(0, (count + GROUP - 1) // GROUP, group, 0)
    total = jnp.sum(col_acc[...], axis=1)
    own[...] = total[:half]
    other[...] = total[half:]
    rows[...] = jnp.max(row_acc[...], axis=1)


def whole_parts(total):
    high = jnp.floor(total * (1.0 / 256.0)) * 256.0
    return high, total - high


def piece_kernel(x, own, arrived, message):
    half = own.shape[0]
    high, low = whole_parts(own[...] + arrived[...])
    counts = jnp.concatenate([high, low], axis=0).astype(BF16)
    for k in range(half):
        message[k, :BLK] = x[...]
        message[k, BLK:] = counts


def scale_kernel(message, scaled, scale):
    half = scaled.shape[0]
    degree = 1.0 + jnp.sum(
        message[:, BLK : BLK + half].astype(F32) + message[:, BLK + half :].astype(F32), axis=0
    )
    factor = lax.rsqrt(degree)
    scale[...] = factor
    turned = lax.dot_general(
        eye(BLK).astype(F32), factor, NT, precision=lax.Precision.HIGHEST, preferred_element_type=F32
    )
    for k in range(half):
        scaled[k] = (message[k, :BLK].astype(F32) * turned[:, k : k + 1]).astype(BF16)


def forward_kernel(info, coords, tiles, own, other, rows, message, features, acc):
    half, row_blocks = own.shape[0], message.shape[0]
    count, parity, diagonal = info[0], info[1], info[2]
    features[:half] = own[...]
    features[half:] = other[...]

    @pl.when(diagonal == 1)
    def _():
        for p in range(row_blocks):
            acc[p] = features[slot_of(parity * row_blocks + p, parity, half)].astype(F32)

    @pl.when(diagonal == 0)
    def _():
        acc[...] = jnp.zeros_like(acc)

    def group(g, carry):
        for u in range(GROUP):
            s = g * GROUP + u
            live = jnp.where(s < count, 1.0, 0.0).astype(F32)
            source = features[slot_of(coords[s, 1], parity, half)]
            product = jnp.dot(tiles[s], source, preferred_element_type=F32)
            acc[coords[s, 0]] += product * live
        return carry

    lax.fori_loop(0, (count + GROUP - 1) // GROUP, group, 0)
    line = lax.broadcasted_iota(jnp.int32, (16, BLK), 0)
    for p in range(row_blocks):
        message[p, :BLK] = acc[p].astype(BF16)
        high, low = whole_parts(rows[p : p + 1])
        extra = jnp.where(line == 0, high, jnp.where(line == 1, low, 0.0))
        message[p, BLK:] = extra.astype(BF16)


def node_kernel(partials, weight, bias, cotangent, activations, sent, grads):
    parts = grads.shape[0]
    chunk = BLK // parts
    total = jnp.sum(partials[...].astype(F32), axis=0)
    summed = total[:BLK]
    degree = 1.0 + total[BLK : BLK + 1] + total[BLK + 1 : BLK + 2]
    scale = jnp.sum(jnp.where(eye(BLK), lax.rsqrt(degree), 0.0), axis=1, keepdims=True)
    high, low = split(summed)
    high, low = high.astype(BF16), low.astype(BF16)
    product = jnp.dot(high, weight[...], preferred_element_type=F32)
    product += jnp.dot(low, weight[...], preferred_element_type=F32)
    pre = scale * product + bias[...]
    sigmoid = jax.nn.sigmoid(pre)
    activations[...] = (pre * sigmoid).astype(BF16)
    grad_pre = cotangent[...].astype(F32) * sigmoid * (1.0 + pre * (1.0 - sigmoid))
    back = (scale * grad_pre).astype(BF16)
    sent[...] = lax.dot_general(weight[...], back, NT, preferred_element_type=F32).astype(BF16)
    grad = lax.dot_general(high, back, TN, preferred_element_type=F32)
    grad += lax.dot_general(low, back, TN, preferred_element_type=F32)
    grad_bias = jnp.sum(grad_pre, axis=0, keepdims=True)
    line = lax.broadcasted_iota(jnp.int32, (8, BLK), 0)
    extra = jnp.where(
        line == 0, grad_bias[:, :BLK], jnp.where(line == 1, grad_bias[:, BLK:], 0.0)
    )
    for k in range(parts):
        grads[k, :chunk] = grad[k * chunk : (k + 1) * chunk, :BLK]
        grads[k, chunk : 2 * chunk] = grad[k * chunk : (k + 1) * chunk, BLK:]
        grads[k, 2 * chunk :] = extra


def mix_kernel(grads, sent, message):
    high, low = split(jnp.sum(grads[...], axis=0))
    tail = jnp.concatenate([high, low], axis=0).astype(BF16)
    for c in range(message.shape[0]):
        message[c, :BLK] = sent[...]
        message[c, BLK:] = tail


def backward_kernel(info, coords, tiles, message, own, other, acc):
    half, row_blocks = own.shape[0], message.shape[0]
    count, parity, diagonal = info[0], info[1], info[2]
    acc[...] = jnp.zeros_like(acc)

    @pl.when(diagonal == 1)
    def _():
        for p in range(row_blocks):
            acc[slot_of(parity * row_blocks + p, parity, half)] = message[p, :BLK].astype(F32)

    def group(g, carry):
        for u in range(GROUP):
            s = g * GROUP + u
            live = jnp.where(s < count, 1.0, 0.0).astype(F32)
            product = jnp.dot(message[coords[s, 0], :BLK], tiles[s], preferred_element_type=F32)
            acc[slot_of(coords[s, 1], parity, half)] += product * live
        return carry

    lax.fori_loop(0, (count + GROUP - 1) // GROUP, group, 0)
    own[...] = acc[:half].astype(BF16)
    for k in range(half):
        other[k * BLK : (k + 1) * BLK] = acc[half + k].astype(BF16)
    tail = jnp.sum(message[:, BLK:].astype(F32), axis=0)
    size = tail.shape[0] // 2
    high, low = split(tail[:size] + tail[size:])
    other[half * BLK :] = jnp.concatenate([high, low], axis=0).astype(BF16)


def pair_kernel(partials, own, arrived, message, grad_bias):
    half = own.shape[0]
    tail = jnp.sum(partials[:, BLK:].astype(F32), axis=0)
    size = tail.shape[0] // 2
    high, low = split(tail[:size] + tail[size:])
    mine = high + low.astype(BF16).astype(F32)
    theirs = arrived[half * BLK :].astype(F32)
    total = mine + theirs[:size] + theirs[size:]
    grad_bias[...] = total[size - 8 :]
    high, low = split(total[: size - 8])
    extra = jnp.concatenate([high, low], axis=0).astype(BF16)
    for k in range(half):
        message[k, :BLK] = (
            own[k].astype(F32) + arrived[k * BLK : (k + 1) * BLK].astype(F32)
        ).astype(BF16)
        message[k, BLK:] = extra


def last_kernel(info, message, scale, grad_inputs, grad_weight):
    half = message.shape[0]
    chunk = BLK // half
    total = jnp.sum(message[:, :BLK].astype(F32), axis=0)
    total = total * scale[pl.ds(info[3], 1), :]
    grad_inputs[...] = total.T.astype(BF16)
    for k in range(half):
        tail = message[k, BLK:].astype(F32)
        tail = tail[: 2 * chunk] + tail[2 * chunk :]
        grad_weight[k * chunk : (k + 1) * chunk, :BLK] = tail[:chunk]
        grad_weight[k * chunk : (k + 1) * chunk, BLK:] = tail[chunk:]


def per_device(node_inputs, weight, bias, edge_tiles, block_coords, block_counts, out_cotangent):
    row_devices = lax.axis_size("row")
    row_blocks = lax.axis_size("col")
    half = row_devices // 2
    slots = edge_tiles.shape[1]
    tiles = edge_tiles[0]
    coords = block_coords[0]
    row_index = lax.axis_index("row")
    col_index = lax.axis_index("col")
    diagonal = (col_index == row_index // (row_devices // row_blocks)).astype(jnp.int32)
    info = jnp.stack([block_counts[0, 0], row_index % 2, diagonal, row_index // 2])
    parities = [[2 * k + h for k in range(half)] for h in range(2)]
    partner = [(i, i ^ 1) for i in range(row_devices)]
    work = 2 * slots * BLK**3

    own_count, other_count, row_count = call(
        count_kernel,
        "count",
        (info, coords, tiles),
        [SMEM, SMEM, VMEM],
        [struct((half, BLK), F32), struct((half, BLK), F32), struct((row_blocks, BLK), F32)],
        [pltpu.VMEM((row_devices, 16, BLK), F32), pltpu.VMEM((row_blocks, 8, BLK), F32)],
        work // 16,
    )
    arrived = lax.ppermute(other_count, "row", partner)
    message = call(
        piece_kernel,
        "piece",
        (node_inputs, own_count, arrived),
        [VMEM] * 3,
        struct((half, BLK + 2 * half, BLK), BF16),
    )
    message = lax.all_to_all(message, "row", 0, 0, tiled=True, axis_index_groups=parities)
    scaled, scale = call(
        scale_kernel,
        "scale",
        (message,),
        [VMEM],
        [struct((half, BLK, BLK), BF16), struct((half, BLK), F32)],
    )
    scaled_other = lax.ppermute(scaled, "row", partner)
    message = call(
        forward_kernel,
        "forward",
        (info, coords, tiles, scaled, scaled_other, row_count),
        [SMEM, SMEM] + [VMEM] * 4,
        struct((row_blocks, BLK + 16, BLK), BF16),
        [pltpu.VMEM((row_devices, BLK, BLK), BF16), pltpu.VMEM((row_blocks, BLK, BLK), F32)],
        work,
    )
    message = lax.all_to_all(message, "col", 0, 0, tiled=True)
    width = weight.shape[1]
    chunk_rows = 2 * (BLK // half) + 8
    activations, sent, grads = call(
        node_kernel,
        "node",
        (message, weight, bias.reshape(1, width), out_cotangent),
        [VMEM] * 4,
        [
            struct((BLK, width), BF16),
            struct((BLK, BLK), BF16),
            struct((half, chunk_rows, BLK), F32),
        ],
        (),
        8 * BLK * BLK * width,
    )
    grads = lax.all_to_all(grads, "row", 0, 0, tiled=True, axis_index_groups=parities)
    message = call(
        mix_kernel,
        "mix",
        (grads, sent),
        [VMEM] * 2,
        struct((row_blocks, BLK + 2 * chunk_rows, BLK), BF16),
    )
    message = lax.all_to_all(message, "col", 0, 0, tiled=True)
    own, other = call(
        backward_kernel,
        "backward",
        (info, coords, tiles, message),
        [SMEM, SMEM, VMEM, VMEM],
        [struct((half, BLK, BLK), BF16), struct((half * BLK + 2 * chunk_rows, BLK), BF16)],
        [pltpu.VMEM((row_devices, BLK, BLK), F32)],
        work,
    )
    arrived = lax.ppermute(other, "row", partner)
    message, grad_bias = call(
        pair_kernel,
        "pair",
        (message, own, arrived),
        [VMEM] * 3,
        [struct((half, BLK + 4 * (BLK // half), BLK), BF16), struct((8, BLK), F32)],
    )
    message = lax.all_to_all(message, "row", 0, 0, tiled=True, axis_index_groups=parities)
    grad_inputs, grad_weight = call(
        last_kernel,
        "last",
        (info, message, scale),
        [SMEM, VMEM, VMEM],
        [struct((BLK, BLK), BF16), struct((BLK, width), F32)],
    )
    return activations, grad_inputs, grad_weight, grad_bias[:2].reshape(width)


def solution(mesh):
    in_specs = (
        P(("col", "row"), None),
        P(),
        P(),
        P("row", "col", None, None),
        P("row", "col", None),
        P("row", "col"),
        P(("row", "col"), None),
    )
    out_specs = (P(("row", "col"), None), P(("col", "row"), None), P(), P())
    return jax.shard_map(
        per_device, mesh=mesh, in_specs=in_specs, out_specs=out_specs, check_vma=False
    )
```

```python
import jax
import jax.numpy as jnp
from jax import lax
from jax.experimental import pallas as pl
from jax.experimental.pallas import tpu as pltpu
from jax.sharding import PartitionSpec as P


BLK = 128
GROUP = 4
UNROLL = 2
PARTS = 4
CODE = 6
MASK = (1 << CODE) - 1
ROW_PAIRS = 4
COL_PAIRS = 3
F32 = jnp.float32
BF16 = jnp.bfloat16
VMEM = pl.BlockSpec(memory_space=pltpu.VMEM)
SMEM = pl.BlockSpec(memory_space=pltpu.SMEM)
NT = (((1,), (1,)), ((), ()))
TN = (((0,), (0,)), ((), ()))


def call(kernel, name, operands, specs, outs, scratch=(), flops=0, limit=32, out_specs=None):
    single = not isinstance(outs, (list, tuple))
    moved = sum(x.size * x.dtype.itemsize for x in operands)
    moved += sum(
        o.dtype.itemsize * _size(o.shape) for o in ([outs] if single else outs)
    )
    return pl.pallas_call(
        kernel,
        out_shape=outs,
        in_specs=specs,
        out_specs=out_specs or (VMEM if single else [VMEM] * len(outs)),
        scratch_shapes=list(scratch),
        compiler_params=pltpu.CompilerParams(vmem_limit_bytes=limit << 20),
        cost_estimate=pl.CostEstimate(flops=flops, bytes_accessed=moved, transcendentals=0),
        name=name,
    )(*operands)


def _size(shape):
    total = 1
    for n in shape:
        total *= n
    return total


def struct(shape, dtype):
    return jax.ShapeDtypeStruct(shape, dtype)


def split(value):
    high = value.astype(BF16).astype(F32)
    return high, value - high


def slot_of(q, parity, half):
    return ((q & 1) ^ parity) * half + (q >> 1)


def eye(n):
    return lax.broadcasted_iota(jnp.int32, (n, n), 0) == lax.broadcasted_iota(jnp.int32, (n, n), 1)


def count_kernel(info, coords, tiles, x, message, held, col_acc, arrivals):
    col_acc[...] = jnp.zeros_like(col_acc)
    count, parity = info[0], info[1]
    half = col_acc.shape[0] // 2
    part = held.shape[0] // PARTS
    copies = [
        pltpu.make_async_copy(
            tiles.at[pl.ds(i * part, part)], held.at[pl.ds(i * part, part)], arrivals.at[i]
        )
        for i in range(PARTS)
    ]
    for copy in copies:
        copy.start()

    def group(g, carry):
        for u in range(UNROLL):
            s = g * UNROLL + u
            live = jnp.where(s < count, 1.0, 0.0).astype(F32)
            column = jnp.sum(held[s].reshape(BLK // 16, 16, BLK), axis=0)
            col_acc[slot_of(coords[s, 1], parity, half)] += column.astype(F32) * live
        return carry

    for i, copy in enumerate(copies):
        copy.wait()
        first = i * part // UNROLL
        last = jnp.minimum((count + UNROLL - 1) // UNROLL, (i + 1) * part // UNROLL)
        lax.fori_loop(first, last, group, 0)
    total = jnp.sum(col_acc[...], axis=1)
    even = jnp.where(parity == 0, total[:half], total[half:])
    odd = jnp.where(parity == 0, total[half:], total[:half])
    total = jnp.concatenate([even, odd], axis=0).astype(BF16)
    for k in range(half):
        message[k, :BLK] = x[...]
        message[k, BLK:] = total


def plan_kernel(info, coords, tiles, rows, plan, row_acc):
    row_blocks = rows.shape[0]
    row_devices = (plan.shape[0] - 2 - row_blocks) // (2 * row_blocks + 1)
    half = row_devices // 2
    second = row_blocks * row_devices
    lengths = 2 * second
    longest = lengths + row_blocks + row_devices
    count, parity = info[0], info[1]

    def blank(i, carry):
        plan[i] = row_devices
        plan[second + i] = row_blocks
        return carry

    lax.fori_loop(0, second, blank, 0, unroll=8)
    for i in range(row_blocks + row_devices + 2):
        plan[lengths + i] = 0

    def enter(s, carry):
        p = coords[s, 0]
        slot = slot_of(coords[s, 1], parity, half)
        at_row, at_col = lengths + p, lengths + row_blocks + slot
        n_row, n_col = plan[at_row], plan[at_col]
        plan[p * row_devices + n_row] = (s << CODE) + slot
        plan[second + slot * row_blocks + n_col] = (s << CODE) + p
        plan[at_row] = n_row + 1
        plan[at_col] = n_col + 1
        return jnp.maximum(carry[0], n_row + 1), jnp.maximum(carry[1], n_col + 1)

    top_row, top_col = lax.fori_loop(0, count, enter, (jnp.int32(0), jnp.int32(0)))
    plan[longest] = top_row
    plan[longest + 1] = top_col

    row_acc[...] = jnp.zeros_like(row_acc)
    ones = jnp.ones((8, BLK), BF16)

    def group(g, carry):
        for u in range(GROUP):
            s = g * GROUP + u
            live = jnp.where(s < count, 1.0, 0.0).astype(F32)
            line = lax.dot_general(ones, tiles[s], NT, preferred_element_type=F32)
            row_acc[coords[s, 0]] += line * live
        return carry

    lax.fori_loop(0, (count + GROUP - 1) // GROUP, group, 0)
    rows[...] = jnp.max(row_acc[...], axis=1)


def whole_parts(total):
    high = jnp.floor(total * (1.0 / 256.0)) * 256.0
    return high, total - high


def forward_kernel(info, plan, tiles, own, other, rows, message, scale, features, acc):
    half, row_blocks = own.shape[0], message.shape[0]
    parity, diagonal = info[1], info[2]
    degree = 1.0 + jnp.sum(own[:, BLK:].astype(F32) + other[:, BLK:].astype(F32), axis=0)
    factor = lax.rsqrt(degree)
    scale[...] = factor
    turned = lax.dot_general(
        eye(BLK).astype(F32), factor, NT, precision=lax.Precision.HIGHEST, preferred_element_type=F32
    )
    even, odd = turned[:, :half], turned[:, half:]
    mine = jnp.where(parity == 0, even, odd)
    theirs = jnp.where(parity == 0, odd, even)
    for k in range(half):
        features[k] = (own[k, :BLK].astype(F32) * mine[:, k : k + 1]).astype(BF16)
        features[half + k] = (other[k, :BLK].astype(F32) * theirs[:, k : k + 1]).astype(BF16)

    row_devices = 2 * half
    features[row_devices] = jnp.zeros((BLK, BLK), BF16)
    lengths = 2 * row_blocks * row_devices

    def pair(p, j):
        first, second = plan[p * row_devices + 2 * j], plan[p * row_devices + 2 * j + 1]
        left = jnp.concatenate([tiles[first >> CODE], tiles[second >> CODE]], axis=1)
        right = jnp.concatenate([features[first & MASK], features[second & MASK]], axis=0)
        return jnp.dot(left, right, preferred_element_type=F32)

    fixed = min(ROW_PAIRS, half)
    for p in range(row_blocks):
        same = features[slot_of(parity * row_blocks + p, parity, half)].astype(F32)
        total = jnp.where(diagonal == 1, same, 0.0)
        for j in range(fixed):
            total += pair(p, j)
        acc[p] = total

    @pl.when(plan[lengths + row_blocks + row_devices] > 2 * fixed)
    def _():
        for p in range(row_blocks):

            def more(j, carry):
                acc[p] += pair(p, j)
                return carry

            lax.fori_loop(fixed, (plan[lengths + p] + 1) // 2, more, 0)

    line = lax.broadcasted_iota(jnp.int32, (16, BLK), 0)
    for p in range(row_blocks):
        message[p, :BLK] = acc[p].astype(BF16)
        high, low = whole_parts(rows[p : p + 1])
        extra = jnp.where(line == 0, high, jnp.where(line == 1, low, 0.0))
        message[p, BLK:] = extra.astype(BF16)


def node_kernel(partials, weight, bias, cotangent, activations, message):
    parts = message.shape[0]
    chunk = BLK // parts
    total = jnp.sum(partials[...].astype(F32), axis=0)
    summed = total[:BLK]
    degree = 1.0 + total[BLK : BLK + 1] + total[BLK + 1 : BLK + 2]
    scale = jnp.sum(jnp.where(eye(BLK), lax.rsqrt(degree), 0.0), axis=1, keepdims=True)
    high, low = split(summed)
    high, low = high.astype(BF16), low.astype(BF16)
    product = jnp.dot(high, weight[...], preferred_element_type=F32)
    product += jnp.dot(low, weight[...], preferred_element_type=F32)
    pre = scale * product + bias[...]
    sigmoid = jax.nn.sigmoid(pre)
    activations[...] = (pre * sigmoid).astype(BF16)
    grad_pre = cotangent[...].astype(F32) * sigmoid * (1.0 + pre * (1.0 - sigmoid))
    back = (scale * grad_pre).astype(BF16)
    sent = lax.dot_general(weight[...], back, NT, preferred_element_type=F32).astype(BF16)
    grad = lax.dot_general(high, back, TN, preferred_element_type=F32)
    grad += lax.dot_general(low, back, TN, preferred_element_type=F32)
    extra = bias_rows(jnp.sum(grad_pre, axis=0, keepdims=True))
    for c in range(parts):
        piece = grad[c * chunk : (c + 1) * chunk]
        message[c, :BLK] = sent
        message[c, BLK : BLK + 2 * chunk] = jnp.concatenate(
            [piece[:, :BLK], piece[:, BLK:]], axis=0
        ).astype(BF16)
        message[c, BLK + 2 * chunk :] = extra


def bias_rows(value):
    line = lax.broadcasted_iota(jnp.int32, (16, BLK), 0)
    high, low = split(value)
    rows = [high[:, :BLK], high[:, BLK:], low[:, :BLK], low[:, BLK:]]
    result = jnp.zeros((16, BLK), F32)
    for i, row in enumerate(rows):
        result = jnp.where(line == i, row, result)
    return result.astype(BF16)


def bias_of(rows):
    return jnp.concatenate([rows[0:1] + rows[2:3], rows[1:2] + rows[3:4]], axis=1)


def backward_half(info, plan, tiles, message, sources, acc, start):
    half, row_blocks = acc.shape[0], message.shape[0]
    row_devices = 2 * half
    parity, diagonal = info[1], info[2]
    second_kind = row_blocks * row_devices
    lengths = 2 * second_kind + row_blocks
    for p in range(row_blocks):
        sources[p] = message[p, :BLK]
    sources[row_blocks] = jnp.zeros((BLK, BLK), BF16)
    acc[...] = jnp.zeros_like(acc)

    @pl.when(diagonal == 1)
    def _():
        shift = parity if start == 0 else 1 - parity
        for i in range(row_blocks // 2):
            p = 2 * i + shift
            acc[slot_of(parity * row_blocks + p, parity, half) - start] = sources[p].astype(F32)

    def pair(k, j):
        at = second_kind + (start + k) * row_blocks + 2 * j
        first, second = plan[at], plan[at + 1]
        left = jnp.concatenate([sources[first & MASK], sources[second & MASK]], axis=1)
        right = jnp.concatenate([tiles[first >> CODE], tiles[second >> CODE]], axis=0)
        return jnp.dot(left, right, preferred_element_type=F32)

    fixed = min(COL_PAIRS, row_blocks // 2)
    for k in range(half):
        total = acc[k]
        for j in range(fixed):
            total += pair(k, j)
        acc[k] = total

    @pl.when(plan[lengths + row_devices + 1] > 2 * fixed)
    def _():
        for k in range(half):

            def more(j, carry):
                acc[k] += pair(k, j)
                return carry

            lax.fori_loop(fixed, (plan[lengths + start + k] + 1) // 2, more, 0)


def backward_other_kernel(info, plan, tiles, message, other, sources, acc):
    half = acc.shape[0]
    backward_half(info, plan, tiles, message, sources, acc, half)
    for k in range(half):
        other[k * BLK : (k + 1) * BLK] = acc[k].astype(BF16)
    tail = jnp.sum(message[:, BLK:].astype(F32), axis=0)
    size = tail.shape[0] - 16
    high, low = split(tail[:size])
    at = half * BLK
    other[at : at + size] = high.astype(BF16)
    other[at + size : at + 2 * size] = low.astype(BF16)
    other[at + 2 * size :] = bias_rows(bias_of(tail[size:]))


def backward_own_kernel(info, plan, tiles, message, own, sources, acc):
    backward_half(info, plan, tiles, message, sources, acc, 0)
    own[...] = acc[...].astype(BF16)


def pair_kernel(partials, own, arrived, message):
    half = own.shape[0]
    tail = jnp.sum(partials[:, BLK:].astype(F32), axis=0)
    size = tail.shape[0] - 16
    at = half * BLK
    theirs = arrived[at:].astype(F32)
    chunk = (tail[:size] + theirs[:size] + theirs[size : 2 * size]).astype(BF16)
    extra = bias_rows(bias_of(tail[size:]) + bias_of(theirs[2 * size :]))
    for k in range(half):
        message[k, :BLK] = (
            own[k].astype(F32) + arrived[k * BLK : (k + 1) * BLK].astype(F32)
        ).astype(BF16)
        message[k, BLK : BLK + size] = chunk
        message[k, BLK + size :] = extra


def tail_kernel(message, chunks, grad_bias):
    tail = jnp.sum(message[:, BLK:].astype(F32), axis=0)
    chunk = (tail.shape[0] - 16) // 2
    piece = jnp.concatenate([tail[:chunk], tail[chunk : 2 * chunk]], axis=1)
    for c in range(chunks.shape[0]):
        chunks[c] = piece
    grad_bias[...] = bias_of(tail[2 * chunk :])


def last_kernel(info, message, scale, grad_inputs):
    total = jnp.sum(message[:, :BLK].astype(F32), axis=0)
    total = total * scale[pl.ds(info[3], 1), :]
    grad_inputs[...] = total.T.astype(BF16)


def per_device(node_inputs, weight, bias, edge_tiles, block_coords, block_counts, out_cotangent):
    row_devices = lax.axis_size("row")
    row_blocks = lax.axis_size("col")
    half = row_devices // 2
    slots = edge_tiles.shape[1]
    tiles = edge_tiles[0]
    coords = block_coords[0]
    row_index = lax.axis_index("row")
    col_index = lax.axis_index("col")
    diagonal = (col_index == row_index // (row_devices // row_blocks)).astype(jnp.int32)
    info = jnp.stack([block_counts[0, 0], row_index % 2, diagonal, row_index % 2 * half + row_index // 2])
    parities = [[2 * k + h for k in range(half)] for h in range(2)]
    partner = [(i, i ^ 1) for i in range(row_devices)]
    work = 2 * slots * BLK**3

    pieces = call(
        count_kernel,
        "count",
        (info, coords, tiles, node_inputs),
        [SMEM, SMEM, pl.BlockSpec(memory_space=pl.ANY), VMEM],
        struct((half, BLK + row_devices, BLK), BF16),
        [
            pltpu.VMEM((slots, BLK, BLK), BF16),
            pltpu.VMEM((row_devices, 16, BLK), F32),
            pltpu.SemaphoreType.DMA((PARTS,)),
        ],
        work // 128,
        56,
    )
    pieces = lax.all_to_all(pieces, "row", 0, 0, tiled=True, axis_index_groups=parities)
    entries = 2 * row_blocks * row_devices + row_blocks + row_devices + 2
    row_count, plan = call(
        plan_kernel,
        "plan",
        (info, coords, tiles),
        [SMEM, SMEM, VMEM],
        [struct((row_blocks, BLK), F32), struct((entries,), jnp.int32)],
        [pltpu.VMEM((row_blocks, 8, BLK), F32)],
        work // 16,
        out_specs=[VMEM, SMEM],
    )
    pieces, row_count = lax.optimization_barrier((pieces, row_count))
    pieces_other = lax.ppermute(pieces, "row", partner)
    message, scale = call(
        forward_kernel,
        "forward",
        (info, plan, tiles, pieces, pieces_other, row_count),
        [SMEM, SMEM] + [VMEM] * 4,
        [struct((row_blocks, BLK + 16, BLK), BF16), struct((row_devices, BLK), F32)],
        [pltpu.VMEM((row_devices + 1, BLK, BLK), BF16), pltpu.VMEM((row_blocks, BLK, BLK), F32)],
        work,
    )
    message = lax.all_to_all(message, "col", 0, 0, tiled=True)
    width = weight.shape[1]
    chunk = BLK // row_blocks
    activations, message = call(
        node_kernel,
        "node",
        (message, weight, bias.reshape(1, width), out_cotangent),
        [VMEM] * 4,
        [
            struct((BLK, width), BF16),
            struct((row_blocks, BLK + 2 * chunk + 16, BLK), BF16),
        ],
        (),
        8 * BLK * BLK * width,
    )
    message = lax.all_to_all(message, "col", 0, 0, tiled=True)
    scratch = [pltpu.VMEM((row_blocks + 1, BLK, BLK), BF16), pltpu.VMEM((half, BLK, BLK), F32)]
    other = call(
        backward_other_kernel,
        "backward_other",
        (info, plan, tiles, message),
        [SMEM, SMEM, VMEM, VMEM],
        struct((half * BLK + 4 * chunk + 16, BLK), BF16),
        scratch,
        work,
    )
    arrived = lax.ppermute(other, "row", partner)
    own = call(
        backward_own_kernel,
        "backward_own",
        (info, plan, tiles, message),
        [SMEM, SMEM, VMEM, VMEM],
        struct((half, BLK, BLK), BF16),
        scratch,
        work,
    )
    message = call(
        pair_kernel,
        "pair",
        (message, own, arrived),
        [VMEM] * 3,
        struct((half, BLK + 2 * chunk + 16, BLK), BF16),
    )
    message = lax.all_to_all(message, "row", 0, 0, tiled=True, axis_index_groups=parities)
    chunks, grad_bias = call(
        tail_kernel,
        "tail",
        (message,),
        [VMEM],
        [struct((row_blocks, chunk, width), F32), struct((1, width), F32)],
    )
    grad_weight = lax.all_to_all(chunks, "col", 0, 0, tiled=True)
    grad_inputs = call(
        last_kernel, "last", (info, message, scale), [SMEM, VMEM, VMEM], struct((BLK, BLK), BF16)
    )
    return activations, grad_inputs, grad_weight.reshape(BLK, width), grad_bias.reshape(width)


def solution(mesh):
    in_specs = (
        P(("col", "row"), None),
        P(),
        P(),
        P("row", "col", None, None),
        P("row", "col", None),
        P("row", "col"),
        P(("row", "col"), None),
    )
    out_specs = (P(("row", "col"), None), P(("col", "row"), None), P(), P())
    return jax.shard_map(
        per_device, mesh=mesh, in_specs=in_specs, out_specs=out_specs, check_vma=False
    )
```

```python
import jax
import jax.numpy as jnp
from jax import lax
from jax.experimental import pallas as pl
from jax.experimental.pallas import tpu as pltpu
from jax.sharding import PartitionSpec as P


BLK = 128
GROUP = 4
TAIL = 8
UNROLL = 2
PARTS = 4
CODE = 6
MASK = (1 << CODE) - 1
ROW_PAIRS = 4
COL_PAIRS = 3
F32 = jnp.float32
BF16 = jnp.bfloat16
VMEM = pl.BlockSpec(memory_space=pltpu.VMEM)
SMEM = pl.BlockSpec(memory_space=pltpu.SMEM)
ANY = pl.BlockSpec(memory_space=pl.ANY)
NT = (((1,), (1,)), ((), ()))
TN = (((0,), (0,)), ((), ()))


def call(kernel, name, operands, specs, outs, scratch=(), flops=0, limit=32, out_specs=None):
    single = not isinstance(outs, (list, tuple))
    moved = sum(x.size * x.dtype.itemsize for x in operands)
    moved += sum(
        o.dtype.itemsize * _size(o.shape) for o in ([outs] if single else outs)
    )
    return pl.pallas_call(
        kernel,
        out_shape=outs,
        in_specs=specs,
        out_specs=out_specs or (VMEM if single else [VMEM] * len(outs)),
        scratch_shapes=list(scratch),
        compiler_params=pltpu.CompilerParams(vmem_limit_bytes=limit << 20),
        cost_estimate=pl.CostEstimate(flops=flops, bytes_accessed=moved, transcendentals=0),
        name=name,
    )(*operands)


def _size(shape):
    total = 1
    for n in shape:
        total *= n
    return total


def struct(shape, dtype):
    return jax.ShapeDtypeStruct(shape, dtype)


def split(value):
    high = value.astype(BF16).astype(F32)
    return high, value - high


def slot_of(q, parity, half):
    return ((q & 1) ^ parity) * half + (q >> 1)


def place(row_devices, row_blocks):
    row, col = lax.axis_index("row"), lax.axis_index("col")
    diagonal = col == row // (row_devices // row_blocks)
    return row & 1, row >> 1, diagonal


def eye(n):
    return lax.broadcasted_iota(jnp.int32, (n, n), 0) == lax.broadcasted_iota(jnp.int32, (n, n), 1)


def count_kernel(live_slots, coords, tiles, x, message, held, col_acc, arrivals):
    col_acc[...] = jnp.zeros_like(col_acc)
    half = col_acc.shape[0] // 2
    count = live_slots[0, 0]
    parity = lax.axis_index("row") & 1
    part = held.shape[0] // PARTS
    copies = [
        pltpu.make_async_copy(
            tiles.at[pl.ds(i * part, part)], held.at[pl.ds(i * part, part)], arrivals.at[i]
        )
        for i in range(PARTS)
    ]
    for copy in copies:
        copy.start()

    def group(g, carry):
        for u in range(UNROLL):
            s = g * UNROLL + u
            live = jnp.where(s < count, 1.0, 0.0).astype(F32)
            column = jnp.sum(held[s].reshape(BLK // 16, 16, BLK), axis=0)
            col_acc[slot_of(coords[1, s], parity, half)] += column.astype(F32) * live
        return carry

    for i, copy in enumerate(copies):
        copy.wait()
        first = i * part // UNROLL
        last = jnp.minimum((count + UNROLL - 1) // UNROLL, (i + 1) * part // UNROLL)
        lax.fori_loop(first, last, group, 0)
    total = jnp.sum(col_acc[...], axis=1)
    even = jnp.where(parity == 0, total[:half], total[half:])
    odd = jnp.where(parity == 0, total[half:], total[:half])
    total = jnp.concatenate([even, odd], axis=0).astype(BF16)
    for k in range(half):
        message[k, :BLK] = x[...]
        message[k, BLK:] = total


def plan_kernel(live_slots, coords, tiles, rows, plan, row_acc):
    row_blocks = rows.shape[0]
    row_devices = (plan.shape[0] - 2 - row_blocks) // (2 * row_blocks + 1)
    half = row_devices // 2
    second = row_blocks * row_devices
    lengths = 2 * second
    longest = lengths + row_blocks + row_devices
    count = live_slots[0, 0]
    parity = lax.axis_index("row") & 1

    def blank(i, carry):
        plan[i] = row_devices
        plan[second + i] = row_blocks
        return carry

    lax.fori_loop(0, second, blank, 0, unroll=8)
    for i in range(row_blocks + row_devices + 2):
        plan[lengths + i] = 0

    def enter(s, carry):
        p = coords[0, s]
        slot = slot_of(coords[1, s], parity, half)
        at_row, at_col = lengths + p, lengths + row_blocks + slot
        n_row, n_col = plan[at_row], plan[at_col]
        plan[p * row_devices + n_row] = (s << CODE) + slot
        plan[second + slot * row_blocks + n_col] = (s << CODE) + p
        plan[at_row] = n_row + 1
        plan[at_col] = n_col + 1
        return jnp.maximum(carry[0], n_row + 1), jnp.maximum(carry[1], n_col + 1)

    top_row, top_col = lax.fori_loop(0, count, enter, (jnp.int32(0), jnp.int32(0)))
    plan[longest] = top_row
    plan[longest + 1] = top_col

    row_acc[...] = jnp.zeros_like(row_acc)
    ones = jnp.ones((8, BLK), BF16)

    def group(g, carry):
        for u in range(GROUP):
            s = g * GROUP + u
            live = jnp.where(s < count, 1.0, 0.0).astype(F32)
            line = lax.dot_general(ones, tiles[s], NT, preferred_element_type=F32)
            row_acc[coords[0, s]] += line * live
        return carry

    lax.fori_loop(0, (count + GROUP - 1) // GROUP, group, 0)
    rows[...] = jnp.max(row_acc[...], axis=1)


def whole_parts(total):
    high = jnp.floor(total * (1.0 / 256.0)) * 256.0
    return high, total - high


def forward_kernel(
    plan, tiles, own, other, rows_in, message, scale_out, features, acc, rows, scale, moved
):
    half, row_blocks = own.shape[0], message.shape[0]
    parity, _, diagonal = place(2 * half, row_blocks)
    arriving = pltpu.make_async_copy(rows_in, rows, moved.at[0])
    arriving.start()
    degree = 1.0 + jnp.sum(own[:, BLK:].astype(F32) + other[:, BLK:].astype(F32), axis=0)
    factor = lax.rsqrt(degree)
    scale[...] = factor
    leaving = pltpu.make_async_copy(scale, scale_out, moved.at[1])
    leaving.start()
    turned = lax.dot_general(
        eye(BLK).astype(F32), factor, NT, precision=lax.Precision.HIGHEST, preferred_element_type=F32
    )
    even, odd = turned[:, :half], turned[:, half:]
    mine = jnp.where(parity == 0, even, odd)
    theirs = jnp.where(parity == 0, odd, even)
    for k in range(half):
        features[k] = (own[k, :BLK].astype(F32) * mine[:, k : k + 1]).astype(BF16)
        features[half + k] = (other[k, :BLK].astype(F32) * theirs[:, k : k + 1]).astype(BF16)

    row_devices = 2 * half
    features[row_devices] = jnp.zeros((BLK, BLK), BF16)
    lengths = 2 * row_blocks * row_devices

    def pair(p, j):
        first, second = plan[p * row_devices + 2 * j], plan[p * row_devices + 2 * j + 1]
        left = jnp.concatenate([tiles[first >> CODE], tiles[second >> CODE]], axis=1)
        right = jnp.concatenate([features[first & MASK], features[second & MASK]], axis=0)
        return jnp.dot(left, right, preferred_element_type=F32)

    fixed = min(ROW_PAIRS, half)
    for p in range(row_blocks):
        same = features[slot_of(parity * row_blocks + p, parity, half)].astype(F32)
        total = jnp.where(diagonal, same, 0.0)
        for j in range(fixed):
            total += pair(p, j)
        acc[p] = total

    @pl.when(plan[lengths + row_blocks + row_devices] > 2 * fixed)
    def _():
        for p in range(row_blocks):

            def more(j, carry):
                acc[p] += pair(p, j)
                return carry

            lax.fori_loop(fixed, (plan[lengths + p] + 1) // 2, more, 0)

    arriving.wait()
    line = lax.broadcasted_iota(jnp.int32, (TAIL, BLK), 0)
    for p in range(row_blocks):
        message[p, :BLK] = acc[p].astype(BF16)
        high, low = whole_parts(rows[p : p + 1])
        extra = jnp.where(line == 0, high, jnp.where(line == 1, low, 0.0))
        message[p, BLK:] = extra.astype(BF16)
    leaving.wait()


def node_kernel(partials, weight, bias, cotangent, activations, message):
    parts = message.shape[0]
    chunk = BLK // parts
    total = jnp.sum(partials[...].astype(F32), axis=0)
    summed = total[:BLK]
    degree = 1.0 + total[BLK : BLK + 1] + total[BLK + 1 : BLK + 2]
    scale = jnp.sum(jnp.where(eye(BLK), lax.rsqrt(degree), 0.0), axis=1, keepdims=True)
    high, low = split(summed)
    high, low = high.astype(BF16), low.astype(BF16)
    product = jnp.dot(high, weight[...], preferred_element_type=F32)
    product += jnp.dot(low, weight[...], preferred_element_type=F32)
    pre = scale * product + bias[...]
    sigmoid = jax.nn.sigmoid(pre)
    activations[...] = (pre * sigmoid).astype(BF16)
    grad_pre = cotangent[...].astype(F32) * sigmoid * (1.0 + pre * (1.0 - sigmoid))
    back = (scale * grad_pre).astype(BF16)
    sent = lax.dot_general(weight[...], back, NT, preferred_element_type=F32).astype(BF16)
    grad = lax.dot_general(high, back, TN, preferred_element_type=F32)
    grad += lax.dot_general(low, back, TN, preferred_element_type=F32)
    extra = bias_rows(jnp.sum(grad_pre, axis=0, keepdims=True))
    for c in range(parts):
        piece = grad[c * chunk : (c + 1) * chunk]
        message[c, :BLK] = sent
        message[c, BLK : BLK + 2 * chunk] = jnp.concatenate(
            [piece[:, :BLK], piece[:, BLK:]], axis=0
        ).astype(BF16)
        message[c, BLK + 2 * chunk :] = extra


def bias_rows(value):
    line = lax.broadcasted_iota(jnp.int32, (TAIL, BLK), 0)
    high, low = split(value)
    rows = [high[:, :BLK], high[:, BLK:], low[:, :BLK], low[:, BLK:]]
    result = jnp.zeros((TAIL, BLK), F32)
    for i, row in enumerate(rows):
        result = jnp.where(line == i, row, result)
    return result.astype(BF16)


def bias_of(rows):
    return jnp.concatenate([rows[0:1] + rows[2:3], rows[1:2] + rows[3:4]], axis=1)


def backward_half(plan, tiles, message, sources, acc, start):
    half, row_blocks = acc.shape[0], message.shape[0]
    row_devices = 2 * half
    parity, _, diagonal = place(row_devices, row_blocks)
    second_kind = row_blocks * row_devices
    lengths = 2 * second_kind + row_blocks
    for p in range(row_blocks):
        sources[p] = message[p, :BLK]
    sources[row_blocks] = jnp.zeros((BLK, BLK), BF16)
    acc[...] = jnp.zeros_like(acc)

    @pl.when(diagonal)
    def _():
        shift = parity if start == 0 else 1 - parity
        for i in range(row_blocks // 2):
            p = 2 * i + shift
            acc[slot_of(parity * row_blocks + p, parity, half) - start] = sources[p].astype(F32)

    def pair(k, j):
        at = second_kind + (start + k) * row_blocks + 2 * j
        first, second = plan[at], plan[at + 1]
        left = jnp.concatenate([sources[first & MASK], sources[second & MASK]], axis=1)
        right = jnp.concatenate([tiles[first >> CODE], tiles[second >> CODE]], axis=0)
        return jnp.dot(left, right, preferred_element_type=F32)

    fixed = min(COL_PAIRS, row_blocks // 2)
    for k in range(half):
        total = acc[k]
        for j in range(fixed):
            total += pair(k, j)
        acc[k] = total

    @pl.when(plan[lengths + row_devices + 1] > 2 * fixed)
    def _():
        for k in range(half):

            def more(j, carry):
                acc[k] += pair(k, j)
                return carry

            lax.fori_loop(fixed, (plan[lengths + start + k] + 1) // 2, more, 0)


def backward_other_kernel(plan, tiles, message, other, sources, acc):
    half = acc.shape[0]
    backward_half(plan, tiles, message, sources, acc, half)
    for k in range(half):
        other[k * BLK : (k + 1) * BLK] = acc[k].astype(BF16)
    tail = jnp.sum(message[:, BLK:].astype(F32), axis=0)
    size = tail.shape[0] - TAIL
    high, low = split(tail[:size])
    at = half * BLK
    other[at : at + size] = high.astype(BF16)
    other[at + size : at + 2 * size] = low.astype(BF16)
    other[at + 2 * size : at + 2 * size + TAIL] = bias_rows(bias_of(tail[size:]))
    other[at + 2 * size + TAIL :] = jnp.zeros((16 - TAIL, BLK), BF16)


def backward_own_kernel(plan, tiles, message, own, sources, acc):
    backward_half(plan, tiles, message, sources, acc, 0)
    own[...] = acc[...].astype(BF16)


def pair_kernel(partials, own, arrived, message):
    half = own.shape[0]
    tail = jnp.sum(partials[:, BLK:].astype(F32), axis=0)
    size = tail.shape[0] - TAIL
    at = half * BLK
    theirs = arrived[at:].astype(F32)
    chunk = (tail[:size] + theirs[:size] + theirs[size : 2 * size]).astype(BF16)
    extra = bias_rows(bias_of(tail[size:]) + bias_of(theirs[2 * size : 2 * size + TAIL]))
    for k in range(half):
        message[k, :BLK] = (
            own[k].astype(F32) + arrived[k * BLK : (k + 1) * BLK].astype(F32)
        ).astype(BF16)
        message[k, BLK : BLK + size] = chunk
        message[k, BLK + size :] = extra


def tail_kernel(message, chunks, grad_bias):
    tail = jnp.sum(message[:, BLK:].astype(F32), axis=0)
    chunk = (tail.shape[0] - TAIL) // 2
    piece = jnp.concatenate([tail[:chunk], tail[chunk : 2 * chunk]], axis=1)
    for c in range(chunks.shape[0]):
        chunks[c] = piece
    grad_bias[...] = bias_of(tail[2 * chunk :])


def last_kernel(message, scale, grad_inputs):
    parity, chip, _ = place(scale.shape[0], scale.shape[0])
    total = jnp.sum(message[:, :BLK].astype(F32), axis=0)
    total = total * scale[pl.ds(parity * message.shape[0] + chip, 1), :]
    grad_inputs[...] = total.T.astype(BF16)


def per_device(node_inputs, weight, bias, edge_tiles, block_coords, block_counts, out_cotangent):
    row_devices = lax.axis_size("row")
    row_blocks = lax.axis_size("col")
    half = row_devices // 2
    slots = edge_tiles.shape[1]
    tiles = edge_tiles[0]
    coords = block_coords[0].T
    parities = [[2 * k + h for k in range(half)] for h in range(2)]
    partner = [(i, i ^ 1) for i in range(row_devices)]
    work = 2 * slots * BLK**3

    pieces = call(
        count_kernel,
        "count",
        (block_counts, coords, tiles, node_inputs),
        [SMEM, SMEM, ANY, VMEM],
        struct((half, BLK + row_devices, BLK), BF16),
        [
            pltpu.VMEM((slots, BLK, BLK), BF16),
            pltpu.VMEM((row_devices, 16, BLK), F32),
            pltpu.SemaphoreType.DMA((PARTS,)),
        ],
        work // 128,
        61,
    )
    pieces = lax.all_to_all(pieces, "row", 0, 0, tiled=True, axis_index_groups=parities)
    entries = 2 * row_blocks * row_devices + row_blocks + row_devices + 2
    row_count, plan = call(
        plan_kernel,
        "plan",
        (block_counts, coords, tiles),
        [SMEM, SMEM, VMEM],
        [struct((row_blocks, BLK), F32), struct((entries,), jnp.int32)],
        [pltpu.VMEM((row_blocks, 8, BLK), F32)],
        work // 16,
        out_specs=[VMEM, SMEM],
    )
    pieces, row_count = lax.optimization_barrier((pieces, row_count))
    pieces_other = lax.ppermute(pieces, "row", partner)
    message, scale = call(
        forward_kernel,
        "forward",
        (plan, tiles, pieces, pieces_other, row_count),
        [SMEM] + [VMEM] * 3 + [ANY],
        [struct((row_blocks, BLK + TAIL, BLK), BF16), struct((row_devices, BLK), F32)],
        [
            pltpu.VMEM((row_devices + 1, BLK, BLK), BF16),
            pltpu.VMEM((row_blocks, BLK, BLK), F32),
            pltpu.VMEM((row_blocks, BLK), F32),
            pltpu.VMEM((row_devices, BLK), F32),
            pltpu.SemaphoreType.DMA((2,)),
        ],
        work,
        out_specs=[VMEM, ANY],
    )
    message = lax.all_to_all(message, "col", 0, 0, tiled=True)
    width = weight.shape[1]
    chunk = BLK // row_blocks
    activations, message = call(
        node_kernel,
        "node",
        (message, weight, bias.reshape(1, width), out_cotangent),
        [VMEM] * 4,
        [
            struct((BLK, width), BF16),
            struct((row_blocks, BLK + 2 * chunk + TAIL, BLK), BF16),
        ],
        (),
        8 * BLK * BLK * width,
    )
    message = lax.all_to_all(message, "col", 0, 0, tiled=True)
    scratch = [pltpu.VMEM((row_blocks + 1, BLK, BLK), BF16), pltpu.VMEM((half, BLK, BLK), F32)]
    other = call(
        backward_other_kernel,
        "backward_other",
        (plan, tiles, message),
        [SMEM, VMEM, VMEM],
        struct((half * BLK + 4 * chunk + 16, BLK), BF16),
        scratch,
        work,
    )
    arrived = lax.ppermute(other, "row", partner)
    own = call(
        backward_own_kernel,
        "backward_own",
        (plan, tiles, message),
        [SMEM, VMEM, VMEM],
        struct((half, BLK, BLK), BF16),
        scratch,
        work,
    )
    message = call(
        pair_kernel,
        "pair",
        (message, own, arrived),
        [VMEM] * 3,
        struct((half, BLK + 2 * chunk + TAIL, BLK), BF16),
    )
    message = lax.all_to_all(message, "row", 0, 0, tiled=True, axis_index_groups=parities)
    chunks, grad_bias = call(
        tail_kernel,
        "tail",
        (message,),
        [VMEM],
        [struct((row_blocks, chunk, width), F32), struct((1, width), F32)],
    )
    grad_weight = lax.all_to_all(chunks, "col", 0, 0, tiled=True)
    grad_inputs = call(
        last_kernel, "last", (message, scale), [VMEM, VMEM], struct((BLK, BLK), BF16)
    )
    return activations, grad_inputs, grad_weight.reshape(BLK, width), grad_bias.reshape(width)


def solution(mesh):
    in_specs = (
        P(("col", "row"), None),
        P(),
        P(),
        P("row", "col", None, None),
        P("row", "col", None),
        P("row", "col"),
        P(("row", "col"), None),
    )
    out_specs = (P(("row", "col"), None), P(("col", "row"), None), P(), P())
    return jax.shard_map(
        per_device, mesh=mesh, in_specs=in_specs, out_specs=out_specs, check_vma=False
    )
```

```python
import jax
import jax.numpy as jnp
from jax import lax
from jax.experimental import pallas as pl
from jax.experimental.pallas import tpu as pltpu
from jax.sharding import PartitionSpec as P


BLK = 128
GROUP = 4
TAIL = 8
UNROLL = 2
PARTS = 4
CODE = 6
MASK = (1 << CODE) - 1
ROW_PAIRS = 4
COL_PAIRS = 3
F32 = jnp.float32
BF16 = jnp.bfloat16
VMEM = pl.BlockSpec(memory_space=pltpu.VMEM)
SMEM = pl.BlockSpec(memory_space=pltpu.SMEM)
ANY = pl.BlockSpec(memory_space=pl.ANY)
NT = (((1,), (1,)), ((), ()))
TN = (((0,), (0,)), ((), ()))


def call(kernel, name, operands, specs, outs, scratch=(), flops=0, limit=32, out_specs=None):
    single = not isinstance(outs, (list, tuple))
    moved = sum(x.size * x.dtype.itemsize for x in operands)
    moved += sum(
        o.dtype.itemsize * _size(o.shape) for o in ([outs] if single else outs)
    )
    return pl.pallas_call(
        kernel,
        out_shape=outs,
        in_specs=specs,
        out_specs=out_specs or (VMEM if single else [VMEM] * len(outs)),
        scratch_shapes=list(scratch),
        compiler_params=pltpu.CompilerParams(vmem_limit_bytes=limit << 20),
        cost_estimate=pl.CostEstimate(flops=flops, bytes_accessed=moved, transcendentals=0),
        name=name,
    )(*operands)


def _size(shape):
    total = 1
    for n in shape:
        total *= n
    return total


def struct(shape, dtype):
    return jax.ShapeDtypeStruct(shape, dtype)


def split(value):
    high = value.astype(BF16).astype(F32)
    return high, value - high


def slot_of(q, parity, half):
    return ((q & 1) ^ parity) * half + (q >> 1)


def place(row_devices, row_blocks):
    row, col = lax.axis_index("row"), lax.axis_index("col")
    diagonal = col == row // (row_devices // row_blocks)
    return row & 1, row >> 1, diagonal


def eye(n):
    return lax.broadcasted_iota(jnp.int32, (n, n), 0) == lax.broadcasted_iota(jnp.int32, (n, n), 1)


def count_kernel(
    live_slots, coords_in, tiles, x_in, message, held, col_acc, x, coords, arrivals, others
):
    half = col_acc.shape[0] // 2
    count = live_slots[0, 0]
    parity = lax.axis_index("row") & 1
    part = held.shape[0] // PARTS
    copies = [
        pltpu.make_async_copy(
            tiles.at[pl.ds(i * part, part)], held.at[pl.ds(i * part, part)], arrivals.at[i]
        )
        for i in range(PARTS)
    ]
    place_copy = pltpu.make_async_copy(coords_in, coords, others.at[0])
    place_copy.start()
    for copy in copies:
        copy.start()
    x_copy = pltpu.make_async_copy(x_in, x, others.at[1])
    x_copy.start()
    col_acc[...] = jnp.zeros_like(col_acc)
    place_copy.wait()
    x_copy.wait()
    for k in range(half):
        message[k, :BLK] = x[...]

    def group(g, carry):
        for u in range(UNROLL):
            s = g * UNROLL + u
            live = jnp.where(s < count, 1.0, 0.0).astype(F32)
            column = jnp.sum(held[s].reshape(BLK // 16, 16, BLK), axis=0)
            col_acc[slot_of(coords[1, s], parity, half)] += column.astype(F32) * live
        return carry

    for i, copy in enumerate(copies):
        copy.wait()
        first = i * part // UNROLL
        last = jnp.minimum((count + UNROLL - 1) // UNROLL, (i + 1) * part // UNROLL)
        lax.fori_loop(first, last, group, 0)
    total = jnp.sum(col_acc[...], axis=1)
    even = jnp.where(parity == 0, total[:half], total[half:])
    odd = jnp.where(parity == 0, total[half:], total[:half])
    total = jnp.concatenate([even, odd], axis=0).astype(BF16)
    for k in range(half):
        message[k, BLK:] = total


def plan_kernel(live_slots, coords, tiles, rows, plan, row_acc):
    row_blocks = rows.shape[0]
    row_devices = (plan.shape[0] - 2 - row_blocks) // (2 * row_blocks + 1)
    half = row_devices // 2
    second = row_blocks * row_devices
    lengths = 2 * second
    longest = lengths + row_blocks + row_devices
    count = live_slots[0, 0]
    parity = lax.axis_index("row") & 1

    def blank(i, carry):
        plan[i] = row_devices
        plan[second + i] = row_blocks
        return carry

    lax.fori_loop(0, second, blank, 0, unroll=8)
    for i in range(row_blocks + row_devices + 2):
        plan[lengths + i] = 0

    def enter(s, carry):
        p = coords[0, s]
        slot = slot_of(coords[1, s], parity, half)
        at_row, at_col = lengths + p, lengths + row_blocks + slot
        n_row, n_col = plan[at_row], plan[at_col]
        plan[p * row_devices + n_row] = (s << CODE) + slot
        plan[second + slot * row_blocks + n_col] = (s << CODE) + p
        plan[at_row] = n_row + 1
        plan[at_col] = n_col + 1
        return jnp.maximum(carry[0], n_row + 1), jnp.maximum(carry[1], n_col + 1)

    top_row, top_col = lax.fori_loop(0, count, enter, (jnp.int32(0), jnp.int32(0)))
    plan[longest] = top_row
    plan[longest + 1] = top_col

    row_acc[...] = jnp.zeros_like(row_acc)
    ones = jnp.ones((8, BLK), BF16)

    def group(g, carry):
        for u in range(GROUP):
            s = g * GROUP + u
            live = jnp.where(s < count, 1.0, 0.0).astype(F32)
            line = lax.dot_general(ones, tiles[s], NT, preferred_element_type=F32)
            row_acc[coords[0, s]] += line * live
        return carry

    lax.fori_loop(0, (count + GROUP - 1) // GROUP, group, 0)
    rows[...] = jnp.max(row_acc[...], axis=1)


def whole_parts(total):
    high = jnp.floor(total * (1.0 / 256.0)) * 256.0
    return high, total - high


def forward_kernel(
    plan, tiles, own, other, rows_in, message, scale_out, features, acc, rows, scale, moved
):
    half, row_blocks = own.shape[0], message.shape[0]
    parity, _, diagonal = place(2 * half, row_blocks)
    arriving = pltpu.make_async_copy(rows_in, rows, moved.at[0])
    arriving.start()
    degree = 1.0 + jnp.sum(own[:, BLK:].astype(F32) + other[:, BLK:].astype(F32), axis=0)
    factor = lax.rsqrt(degree)
    scale[...] = factor
    leaving = pltpu.make_async_copy(scale, scale_out, moved.at[1])
    leaving.start()
    turned = factor.T
    even, odd = turned[:, :half], turned[:, half:]
    mine = jnp.where(parity == 0, even, odd)
    theirs = jnp.where(parity == 0, odd, even)
    for k in range(half):
        features[k] = (own[k, :BLK].astype(F32) * mine[:, k : k + 1]).astype(BF16)
        features[half + k] = (other[k, :BLK].astype(F32) * theirs[:, k : k + 1]).astype(BF16)

    row_devices = 2 * half
    features[row_devices] = jnp.zeros((BLK, BLK), BF16)
    lengths = 2 * row_blocks * row_devices

    def pair(p, j):
        first, second = plan[p * row_devices + 2 * j], plan[p * row_devices + 2 * j + 1]
        left = jnp.concatenate([tiles[first >> CODE], tiles[second >> CODE]], axis=1)
        right = jnp.concatenate([features[first & MASK], features[second & MASK]], axis=0)
        return jnp.dot(left, right, preferred_element_type=F32)

    fixed = min(ROW_PAIRS, half)
    for p in range(row_blocks):
        same = features[slot_of(parity * row_blocks + p, parity, half)].astype(F32)
        total = jnp.where(diagonal, same, 0.0)
        for j in range(fixed):
            total += pair(p, j)
        acc[p] = total

    @pl.when(plan[lengths + row_blocks + row_devices] > 2 * fixed)
    def _():
        for p in range(row_blocks):

            def more(j, carry):
                acc[p] += pair(p, j)
                return carry

            lax.fori_loop(fixed, (plan[lengths + p] + 1) // 2, more, 0)

    arriving.wait()
    line = lax.broadcasted_iota(jnp.int32, (TAIL, BLK), 0)
    for p in range(row_blocks):
        message[p, :BLK] = acc[p].astype(BF16)
        high, low = whole_parts(rows[p : p + 1])
        extra = jnp.where(line == 0, high, jnp.where(line == 1, low, 0.0))
        message[p, BLK:] = extra.astype(BF16)
    leaving.wait()


def node_kernel(partials, weight, bias, cotangent, activations, message):
    parts = message.shape[0]
    chunk = BLK // parts
    total = jnp.sum(partials[...].astype(F32), axis=0)
    summed = total[:BLK]
    degree = 1.0 + total[BLK : BLK + 1] + total[BLK + 1 : BLK + 2]
    scale = jnp.sum(jnp.where(eye(BLK), lax.rsqrt(degree), 0.0), axis=1, keepdims=True)
    high, low = split(summed)
    high, low = high.astype(BF16), low.astype(BF16)
    product = jnp.dot(high, weight[...], preferred_element_type=F32)
    product += jnp.dot(low, weight[...], preferred_element_type=F32)
    pre = scale * product + bias[...]
    sigmoid = jax.nn.sigmoid(pre)
    activations[...] = (pre * sigmoid).astype(BF16)
    grad_pre = cotangent[...].astype(F32) * sigmoid * (1.0 + pre * (1.0 - sigmoid))
    back = (scale * grad_pre).astype(BF16)
    sent = lax.dot_general(weight[...], back, NT, preferred_element_type=F32).astype(BF16)
    grad = lax.dot_general(high, back, TN, preferred_element_type=F32)
    grad += lax.dot_general(low, back, TN, preferred_element_type=F32)
    extra = bias_rows(jnp.sum(grad_pre, axis=0, keepdims=True))
    for c in range(parts):
        piece = grad[c * chunk : (c + 1) * chunk]
        message[c, :BLK] = sent
        message[c, BLK : BLK + 2 * chunk] = jnp.concatenate(
            [piece[:, :BLK], piece[:, BLK:]], axis=0
        ).astype(BF16)
        message[c, BLK + 2 * chunk :] = extra


def bias_rows(value):
    line = lax.broadcasted_iota(jnp.int32, (TAIL, BLK), 0)
    high, low = split(value)
    rows = [high[:, :BLK], high[:, BLK:], low[:, :BLK], low[:, BLK:]]
    result = jnp.zeros((TAIL, BLK), F32)
    for i, row in enumerate(rows):
        result = jnp.where(line == i, row, result)
    return result.astype(BF16)


def bias_of(rows):
    return jnp.concatenate([rows[0:1] + rows[2:3], rows[1:2] + rows[3:4]], axis=1)


def backward_half(plan, tiles, message, sources, acc, start):
    half, row_blocks = acc.shape[0], message.shape[0]
    row_devices = 2 * half
    parity, _, diagonal = place(row_devices, row_blocks)
    second_kind = row_blocks * row_devices
    lengths = 2 * second_kind + row_blocks
    for p in range(row_blocks):
        sources[p] = message[p, :BLK]
    sources[row_blocks] = jnp.zeros((BLK, BLK), BF16)
    acc[...] = jnp.zeros_like(acc)

    @pl.when(diagonal)
    def _():
        shift = parity if start == 0 else 1 - parity
        for i in range(row_blocks // 2):
            p = 2 * i + shift
            acc[slot_of(parity * row_blocks + p, parity, half) - start] = sources[p].astype(F32)

    def pair(k, j):
        at = second_kind + (start + k) * row_blocks + 2 * j
        first, second = plan[at], plan[at + 1]
        left = jnp.concatenate([sources[first & MASK], sources[second & MASK]], axis=1)
        right = jnp.concatenate([tiles[first >> CODE], tiles[second >> CODE]], axis=0)
        return jnp.dot(left, right, preferred_element_type=F32)

    fixed = min(COL_PAIRS, row_blocks // 2)
    for k in range(half):
        total = acc[k]
        for j in range(fixed):
            total += pair(k, j)
        acc[k] = total

    @pl.when(plan[lengths + row_devices + 1] > 2 * fixed)
    def _():
        for k in range(half):

            def more(j, carry):
                acc[k] += pair(k, j)
                return carry

            lax.fori_loop(fixed, (plan[lengths + start + k] + 1) // 2, more, 0)


def backward_other_kernel(plan, tiles, message, other, sources, acc):
    half = acc.shape[0]
    backward_half(plan, tiles, message, sources, acc, half)
    for k in range(half):
        other[k * BLK : (k + 1) * BLK] = acc[k].astype(BF16)
    tail = jnp.sum(message[:, BLK:].astype(F32), axis=0)
    size = tail.shape[0] - TAIL
    high, low = split(tail[:size])
    at = half * BLK
    other[at : at + size] = high.astype(BF16)
    other[at + size : at + 2 * size] = low.astype(BF16)
    other[at + 2 * size : at + 2 * size + TAIL] = bias_rows(bias_of(tail[size:]))
    other[at + 2 * size + TAIL :] = jnp.zeros((16 - TAIL, BLK), BF16)


def backward_own_kernel(plan, tiles, message, own, sources, acc):
    backward_half(plan, tiles, message, sources, acc, 0)
    own[...] = acc[...].astype(BF16)


def pair_kernel(partials, own, arrived, message):
    half = own.shape[0]
    tail = jnp.sum(partials[:, BLK:].astype(F32), axis=0)
    size = tail.shape[0] - TAIL
    at = half * BLK
    theirs = arrived[at:].astype(F32)
    chunk = (tail[:size] + theirs[:size] + theirs[size : 2 * size]).astype(BF16)
    extra = bias_rows(bias_of(tail[size:]) + bias_of(theirs[2 * size : 2 * size + TAIL]))
    for k in range(half):
        message[k, :BLK] = (
            own[k].astype(F32) + arrived[k * BLK : (k + 1) * BLK].astype(F32)
        ).astype(BF16)
        message[k, BLK : BLK + size] = chunk
        message[k, BLK + size :] = extra


def tail_kernel(message, chunks, grad_bias):
    tail = jnp.sum(message[:, BLK:].astype(F32), axis=0)
    chunk = (tail.shape[0] - TAIL) // 2
    piece = jnp.concatenate([tail[:chunk], tail[chunk : 2 * chunk]], axis=1)
    for c in range(chunks.shape[0]):
        chunks[c] = piece
    grad_bias[...] = bias_of(tail[2 * chunk :])


def last_kernel(message, scale, grad_inputs):
    parity, chip, _ = place(scale.shape[0], scale.shape[0])
    total = jnp.sum(message[:, :BLK].astype(F32), axis=0)
    total = total * scale[pl.ds(parity * message.shape[0] + chip, 1), :]
    grad_inputs[...] = total.T.astype(BF16)


def per_device(node_inputs, weight, bias, edge_tiles, block_coords, block_counts, out_cotangent):
    row_devices = lax.axis_size("row")
    row_blocks = lax.axis_size("col")
    half = row_devices // 2
    slots = edge_tiles.shape[1]
    tiles = edge_tiles[0]
    coords = block_coords[0].T
    parities = [[2 * k + h for k in range(half)] for h in range(2)]
    partner = [(i, i ^ 1) for i in range(row_devices)]
    work = 2 * slots * BLK**3

    pieces = call(
        count_kernel,
        "count",
        (block_counts, coords, tiles, node_inputs),
        [SMEM, ANY, ANY, ANY],
        struct((half, BLK + row_devices, BLK), BF16),
        [
            pltpu.VMEM((slots, BLK, BLK), BF16),
            pltpu.VMEM((row_devices, 16, BLK), F32),
            pltpu.VMEM((BLK, BLK), BF16),
            pltpu.SMEM((2, slots), jnp.int32),
            pltpu.SemaphoreType.DMA((PARTS,)),
            pltpu.SemaphoreType.DMA((2,)),
        ],
        work // 128,
        61,
    )
    pieces = lax.all_to_all(pieces, "row", 0, 0, tiled=True, axis_index_groups=parities)
    entries = 2 * row_blocks * row_devices + row_blocks + row_devices + 2
    row_count, plan = call(
        plan_kernel,
        "plan",
        (block_counts, coords, tiles),
        [SMEM, SMEM, VMEM],
        [struct((row_blocks, BLK), F32), struct((entries,), jnp.int32)],
        [pltpu.VMEM((row_blocks, 8, BLK), F32)],
        work // 16,
        out_specs=[VMEM, SMEM],
    )
    pieces, row_count = lax.optimization_barrier((pieces, row_count))
    pieces_other = lax.ppermute(pieces, "row", partner)
    message, scale = call(
        forward_kernel,
        "forward",
        (plan, tiles, pieces, pieces_other, row_count),
        [SMEM] + [VMEM] * 3 + [ANY],
        [struct((row_blocks, BLK + TAIL, BLK), BF16), struct((row_devices, BLK), F32)],
        [
            pltpu.VMEM((row_devices + 1, BLK, BLK), BF16),
            pltpu.VMEM((row_blocks, BLK, BLK), F32),
            pltpu.VMEM((row_blocks, BLK), F32),
            pltpu.VMEM((row_devices, BLK), F32),
            pltpu.SemaphoreType.DMA((2,)),
        ],
        work,
        out_specs=[VMEM, ANY],
    )
    message = lax.all_to_all(message, "col", 0, 0, tiled=True)
    width = weight.shape[1]
    chunk = BLK // row_blocks
    activations, message = call(
        node_kernel,
        "node",
        (message, weight, bias.reshape(1, width), out_cotangent),
        [VMEM] * 4,
        [
            struct((BLK, width), BF16),
            struct((row_blocks, BLK + 2 * chunk + TAIL, BLK), BF16),
        ],
        (),
        8 * BLK * BLK * width,
    )
    message = lax.all_to_all(message, "col", 0, 0, tiled=True)
    scratch = [pltpu.VMEM((row_blocks + 1, BLK, BLK), BF16), pltpu.VMEM((half, BLK, BLK), F32)]
    other = call(
        backward_other_kernel,
        "backward_other",
        (plan, tiles, message),
        [SMEM, VMEM, VMEM],
        struct((half * BLK + 4 * chunk + 16, BLK), BF16),
        scratch,
        work,
    )
    arrived = lax.ppermute(other, "row", partner)
    own = call(
        backward_own_kernel,
        "backward_own",
        (plan, tiles, message),
        [SMEM, VMEM, VMEM],
        struct((half, BLK, BLK), BF16),
        scratch,
        work,
    )
    message = call(
        pair_kernel,
        "pair",
        (message, own, arrived),
        [VMEM] * 3,
        struct((half, BLK + 2 * chunk + TAIL, BLK), BF16),
    )
    message = lax.all_to_all(message, "row", 0, 0, tiled=True, axis_index_groups=parities)
    chunks, grad_bias = call(
        tail_kernel,
        "tail",
        (message,),
        [VMEM],
        [struct((row_blocks, chunk, width), F32), struct((1, width), F32)],
    )
    grad_weight = lax.all_to_all(chunks, "col", 0, 0, tiled=True)
    grad_inputs = call(
        last_kernel, "last", (message, scale), [VMEM, VMEM], struct((BLK, BLK), BF16)
    )
    return activations, grad_inputs, grad_weight.reshape(BLK, width), grad_bias.reshape(width)


def solution(mesh):
    in_specs = (
        P(("col", "row"), None),
        P(),
        P(),
        P("row", "col", None, None),
        P("row", "col", None),
        P("row", "col"),
        P(("row", "col"), None),
    )
    out_specs = (P(("row", "col"), None), P(("col", "row"), None), P(), P())
    return jax.shard_map(
        per_device, mesh=mesh, in_specs=in_specs, out_specs=out_specs, check_vma=False
    )
```

```python
import jax
import jax.numpy as jnp
from jax import lax
from jax.experimental import pallas as pl
from jax.experimental.pallas import tpu as pltpu
from jax.sharding import PartitionSpec as P


BLK = 128
GROUP = 4
TAIL = 8
UNROLL = 2
PARTS = 4
CODE = 6
MASK = (1 << CODE) - 1
ROW_PAIRS = 4
COL_PAIRS = 3
F32 = jnp.float32
BF16 = jnp.bfloat16
VMEM = pl.BlockSpec(memory_space=pltpu.VMEM)
SMEM = pl.BlockSpec(memory_space=pltpu.SMEM)
ANY = pl.BlockSpec(memory_space=pl.ANY)
NT = (((1,), (1,)), ((), ()))
TN = (((0,), (0,)), ((), ()))


def call(kernel, name, operands, specs, outs, scratch=(), flops=0, limit=32, out_specs=None):
    single = not isinstance(outs, (list, tuple))
    moved = sum(x.size * x.dtype.itemsize for x in operands)
    moved += sum(
        o.dtype.itemsize * _size(o.shape) for o in ([outs] if single else outs)
    )
    return pl.pallas_call(
        kernel,
        out_shape=outs,
        in_specs=specs,
        out_specs=out_specs or (VMEM if single else [VMEM] * len(outs)),
        scratch_shapes=list(scratch),
        compiler_params=pltpu.CompilerParams(vmem_limit_bytes=limit << 20),
        cost_estimate=pl.CostEstimate(flops=flops, bytes_accessed=moved, transcendentals=0),
        name=name,
    )(*operands)


def _size(shape):
    total = 1
    for n in shape:
        total *= n
    return total


def struct(shape, dtype):
    return jax.ShapeDtypeStruct(shape, dtype)


def split(value):
    high = value.astype(BF16).astype(F32)
    return high, value - high


def slot_of(q, parity, half):
    return ((q & 1) ^ parity) * half + (q >> 1)


def place(row_devices, row_blocks):
    row, col = lax.axis_index("row"), lax.axis_index("col")
    diagonal = col == row // (row_devices // row_blocks)
    return row & 1, row >> 1, diagonal


def eye(n):
    return lax.broadcasted_iota(jnp.int32, (n, n), 0) == lax.broadcasted_iota(jnp.int32, (n, n), 1)


def count_kernel(
    live_slots, coords_in, tiles, x_in, message, held, col_acc, x, coords, arrivals, others
):
    half = col_acc.shape[0] // 2
    count = live_slots[0, 0]
    parity = lax.axis_index("row") & 1
    part = held.shape[0] // PARTS
    copies = [
        pltpu.make_async_copy(
            tiles.at[pl.ds(i * part, part)], held.at[pl.ds(i * part, part)], arrivals.at[i]
        )
        for i in range(PARTS)
    ]
    place_copy = pltpu.make_async_copy(coords_in, coords, others.at[0])
    place_copy.start()
    for copy in copies:
        copy.start()
    x_copy = pltpu.make_async_copy(x_in, x, others.at[1])
    x_copy.start()
    col_acc[...] = jnp.zeros_like(col_acc)
    place_copy.wait()
    x_copy.wait()
    for k in range(half):
        message[k, :BLK] = x[...]

    def group(g, carry):
        for u in range(UNROLL):
            s = g * UNROLL + u
            live = jnp.where(s < count, 1.0, 0.0).astype(F32)
            column = jnp.sum(held[s].reshape(BLK // 16, 16, BLK), axis=0)
            col_acc[slot_of(coords[1, s], parity, half)] += column.astype(F32) * live
        return carry

    for i, copy in enumerate(copies):
        copy.wait()
        first = i * part // UNROLL
        last = jnp.minimum((count + UNROLL - 1) // UNROLL, (i + 1) * part // UNROLL)
        lax.fori_loop(first, last, group, 0)
    total = jnp.sum(col_acc[...], axis=1)
    even = jnp.where(parity == 0, total[:half], total[half:])
    odd = jnp.where(parity == 0, total[half:], total[:half])
    total = jnp.concatenate([even, odd], axis=0).astype(BF16)
    for k in range(half):
        message[k, BLK:] = total


def plan_kernel(live_slots, coords, tiles, rows, plan, row_acc):
    row_blocks = rows.shape[0]
    row_devices = (plan.shape[0] - 2 - row_blocks) // (2 * row_blocks + 1)
    half = row_devices // 2
    second = row_blocks * row_devices
    lengths = 2 * second
    longest = lengths + row_blocks + row_devices
    count = live_slots[0, 0]
    parity = lax.axis_index("row") & 1

    def blank(i, carry):
        plan[i] = row_devices
        plan[second + i] = row_blocks
        return carry

    lax.fori_loop(0, second, blank, 0, unroll=8)
    for i in range(row_blocks + row_devices + 2):
        plan[lengths + i] = 0

    def enter(s, carry):
        p = coords[0, s]
        slot = slot_of(coords[1, s], parity, half)
        at_row, at_col = lengths + p, lengths + row_blocks + slot
        n_row, n_col = plan[at_row], plan[at_col]
        plan[p * row_devices + n_row] = (s << CODE) + slot
        plan[second + slot * row_blocks + n_col] = (s << CODE) + p
        plan[at_row] = n_row + 1
        plan[at_col] = n_col + 1
        return jnp.maximum(carry[0], n_row + 1), jnp.maximum(carry[1], n_col + 1)

    top_row, top_col = lax.fori_loop(0, count, enter, (jnp.int32(0), jnp.int32(0)))
    plan[longest] = top_row
    plan[longest + 1] = top_col

    row_acc[...] = jnp.zeros_like(row_acc)
    ones = jnp.ones((8, BLK), BF16)

    def group(g, carry):
        for u in range(GROUP):
            s = g * GROUP + u
            live = jnp.where(s < count, 1.0, 0.0).astype(F32)
            line = lax.dot_general(ones, tiles[s], NT, preferred_element_type=F32)
            row_acc[coords[0, s]] += line * live
        return carry

    lax.fori_loop(0, (count + GROUP - 1) // GROUP, group, 0)
    rows[...] = jnp.max(row_acc[...], axis=1)


def whole_parts(total):
    high = jnp.floor(total * (1.0 / 256.0)) * 256.0
    return high, total - high


def forward_kernel(
    plan, tiles, own, other, rows_in, message, scale_out, features, acc, rows, scale, moved
):
    half, row_blocks = own.shape[0], message.shape[0]
    parity, _, diagonal = place(2 * half, row_blocks)
    arriving = pltpu.make_async_copy(rows_in, rows, moved.at[0])
    arriving.start()
    degree = 1.0 + jnp.sum(own[:, BLK:].astype(F32) + other[:, BLK:].astype(F32), axis=0)
    factor = lax.rsqrt(degree)
    scale[...] = factor
    leaving = pltpu.make_async_copy(scale, scale_out, moved.at[1])
    leaving.start()
    turned = factor.T
    even, odd = turned[:, :half], turned[:, half:]
    mine = jnp.where(parity == 0, even, odd)
    theirs = jnp.where(parity == 0, odd, even)
    for k in range(half):
        features[k] = (own[k, :BLK].astype(F32) * mine[:, k : k + 1]).astype(BF16)
        features[half + k] = (other[k, :BLK].astype(F32) * theirs[:, k : k + 1]).astype(BF16)

    row_devices = 2 * half
    features[row_devices] = jnp.zeros((BLK, BLK), BF16)
    lengths = 2 * row_blocks * row_devices

    def pair(p, j):
        first, second = plan[p * row_devices + 2 * j], plan[p * row_devices + 2 * j + 1]
        left = jnp.concatenate([tiles[first >> CODE], tiles[second >> CODE]], axis=1)
        right = jnp.concatenate([features[first & MASK], features[second & MASK]], axis=0)
        return jnp.dot(left, right, preferred_element_type=F32)

    fixed = min(ROW_PAIRS, half)
    for p in range(row_blocks):
        same = features[slot_of(parity * row_blocks + p, parity, half)].astype(F32)
        total = jnp.where(diagonal, same, 0.0)
        for j in range(fixed):
            total += pair(p, j)
        acc[p] = total
        message[p, :BLK] = total.astype(BF16)

    @pl.when(plan[lengths + row_blocks + row_devices] > 2 * fixed)
    def _():
        for p in range(row_blocks):

            def more(j, carry):
                acc[p] += pair(p, j)
                return carry

            lax.fori_loop(fixed, (plan[lengths + p] + 1) // 2, more, 0)
            message[p, :BLK] = acc[p].astype(BF16)

    arriving.wait()
    line = lax.broadcasted_iota(jnp.int32, (TAIL, BLK), 0)
    for p in range(row_blocks):
        high, low = whole_parts(rows[p : p + 1])
        extra = jnp.where(line == 0, high, jnp.where(line == 1, low, 0.0))
        message[p, BLK:] = extra.astype(BF16)
    leaving.wait()


def node_kernel(partials, weight, bias, cotangent, activations, message):
    parts = message.shape[0]
    chunk = BLK // parts
    total = jnp.sum(partials[...].astype(F32), axis=0)
    summed = total[:BLK]
    degree = 1.0 + total[BLK : BLK + 1] + total[BLK + 1 : BLK + 2]
    scale = jnp.sum(jnp.where(eye(BLK), lax.rsqrt(degree), 0.0), axis=1, keepdims=True)
    high, low = split(summed)
    high, low = high.astype(BF16), low.astype(BF16)
    product = jnp.dot(high, weight[...], preferred_element_type=F32)
    product += jnp.dot(low, weight[...], preferred_element_type=F32)
    pre = scale * product + bias[...]
    sigmoid = jax.nn.sigmoid(pre)
    activations[...] = (pre * sigmoid).astype(BF16)
    grad_pre = cotangent[...].astype(F32) * sigmoid * (1.0 + pre * (1.0 - sigmoid))
    back = (scale * grad_pre).astype(BF16)
    sent = lax.dot_general(weight[...], back, NT, preferred_element_type=F32).astype(BF16)
    grad = lax.dot_general(high, back, TN, preferred_element_type=F32)
    grad += lax.dot_general(low, back, TN, preferred_element_type=F32)
    extra = bias_rows(jnp.sum(grad_pre, axis=0, keepdims=True))
    for c in range(parts):
        piece = grad[c * chunk : (c + 1) * chunk]
        message[c, :BLK] = sent
        message[c, BLK : BLK + 2 * chunk] = jnp.concatenate(
            [piece[:, :BLK], piece[:, BLK:]], axis=0
        ).astype(BF16)
        message[c, BLK + 2 * chunk :] = extra


def bias_rows(value):
    line = lax.broadcasted_iota(jnp.int32, (TAIL, BLK), 0)
    high, low = split(value)
    rows = [high[:, :BLK], high[:, BLK:], low[:, :BLK], low[:, BLK:]]
    result = jnp.zeros((TAIL, BLK), F32)
    for i, row in enumerate(rows):
        result = jnp.where(line == i, row, result)
    return result.astype(BF16)


def bias_of(rows):
    return jnp.concatenate([rows[0:1] + rows[2:3], rows[1:2] + rows[3:4]], axis=1)


def backward_half(plan, tiles, message, sources, acc, start):
    half, row_blocks = acc.shape[0], message.shape[0]
    row_devices = 2 * half
    parity, _, diagonal = place(row_devices, row_blocks)
    second_kind = row_blocks * row_devices
    lengths = 2 * second_kind + row_blocks
    for p in range(row_blocks):
        sources[p] = message[p, :BLK]
    sources[row_blocks] = jnp.zeros((BLK, BLK), BF16)
    acc[...] = jnp.zeros_like(acc)

    @pl.when(diagonal)
    def _():
        shift = parity if start == 0 else 1 - parity
        for i in range(row_blocks // 2):
            p = 2 * i + shift
            acc[slot_of(parity * row_blocks + p, parity, half) - start] = sources[p].astype(F32)

    def pair(k, j):
        at = second_kind + (start + k) * row_blocks + 2 * j
        first, second = plan[at], plan[at + 1]
        left = jnp.concatenate([sources[first & MASK], sources[second & MASK]], axis=1)
        right = jnp.concatenate([tiles[first >> CODE], tiles[second >> CODE]], axis=0)
        return jnp.dot(left, right, preferred_element_type=F32)

    fixed = min(COL_PAIRS, row_blocks // 2)
    for k in range(half):
        total = acc[k]
        for j in range(fixed):
            total += pair(k, j)
        acc[k] = total

    @pl.when(plan[lengths + row_devices + 1] > 2 * fixed)
    def _():
        for k in range(half):

            def more(j, carry):
                acc[k] += pair(k, j)
                return carry

            lax.fori_loop(fixed, (plan[lengths + start + k] + 1) // 2, more, 0)


def backward_other_kernel(plan, tiles, message, other, sources, acc):
    half = acc.shape[0]
    backward_half(plan, tiles, message, sources, acc, half)
    for k in range(half):
        other[k * BLK : (k + 1) * BLK] = acc[k].astype(BF16)
    tail = jnp.sum(message[:, BLK:].astype(F32), axis=0)
    size = tail.shape[0] - TAIL
    high, low = split(tail[:size])
    at = half * BLK
    other[at : at + size] = high.astype(BF16)
    other[at + size : at + 2 * size] = low.astype(BF16)
    other[at + 2 * size : at + 2 * size + TAIL] = bias_rows(bias_of(tail[size:]))
    other[at + 2 * size + TAIL :] = jnp.zeros((16 - TAIL, BLK), BF16)


def backward_own_kernel(plan, tiles, message, own, sources, acc):
    backward_half(plan, tiles, message, sources, acc, 0)
    own[...] = acc[...].astype(BF16)


def pair_kernel(partials, own, arrived, message):
    half = own.shape[0]
    tail = jnp.sum(partials[:, BLK:].astype(F32), axis=0)
    size = tail.shape[0] - TAIL
    at = half * BLK
    theirs = arrived[at:].astype(F32)
    chunk = (tail[:size] + theirs[:size] + theirs[size : 2 * size]).astype(BF16)
    extra = bias_rows(bias_of(tail[size:]) + bias_of(theirs[2 * size : 2 * size + TAIL]))
    for k in range(half):
        message[k, :BLK] = (
            own[k].astype(F32) + arrived[k * BLK : (k + 1) * BLK].astype(F32)
        ).astype(BF16)
        message[k, BLK : BLK + size] = chunk
        message[k, BLK + size :] = extra


def tail_kernel(message, chunks, grad_bias):
    tail = jnp.sum(message[:, BLK:].astype(F32), axis=0)
    chunk = (tail.shape[0] - TAIL) // 2
    piece = jnp.concatenate([tail[:chunk], tail[chunk : 2 * chunk]], axis=1)
    for c in range(chunks.shape[0]):
        chunks[c] = piece
    grad_bias[...] = bias_of(tail[2 * chunk :])


def last_kernel(message, scale, grad_inputs):
    parity, chip, _ = place(scale.shape[0], scale.shape[0])
    total = jnp.sum(message[:, :BLK].astype(F32), axis=0)
    total = total * scale[pl.ds(parity * message.shape[0] + chip, 1), :]
    grad_inputs[...] = total.T.astype(BF16)


def per_device(node_inputs, weight, bias, edge_tiles, block_coords, block_counts, out_cotangent):
    row_devices = lax.axis_size("row")
    row_blocks = lax.axis_size("col")
    half = row_devices // 2
    slots = edge_tiles.shape[1]
    tiles = edge_tiles[0]
    coords = block_coords[0].T
    parities = [[2 * k + h for k in range(half)] for h in range(2)]
    partner = [(i, i ^ 1) for i in range(row_devices)]
    work = 2 * slots * BLK**3

    pieces = call(
        count_kernel,
        "count",
        (block_counts, coords, tiles, node_inputs),
        [SMEM, ANY, ANY, ANY],
        struct((half, BLK + row_devices, BLK), BF16),
        [
            pltpu.VMEM((slots, BLK, BLK), BF16),
            pltpu.VMEM((row_devices, 16, BLK), F32),
            pltpu.VMEM((BLK, BLK), BF16),
            pltpu.SMEM((2, slots), jnp.int32),
            pltpu.SemaphoreType.DMA((PARTS,)),
            pltpu.SemaphoreType.DMA((2,)),
        ],
        work // 128,
        61,
    )
    pieces = lax.all_to_all(pieces, "row", 0, 0, tiled=True, axis_index_groups=parities)
    entries = 2 * row_blocks * row_devices + row_blocks + row_devices + 2
    row_count, plan = call(
        plan_kernel,
        "plan",
        (block_counts, coords, tiles),
        [SMEM, SMEM, VMEM],
        [struct((row_blocks, BLK), F32), struct((entries,), jnp.int32)],
        [pltpu.VMEM((row_blocks, 8, BLK), F32)],
        work // 16,
        out_specs=[VMEM, SMEM],
    )
    pieces, row_count = lax.optimization_barrier((pieces, row_count))
    pieces_other = lax.ppermute(pieces, "row", partner)
    message, scale = call(
        forward_kernel,
        "forward",
        (plan, tiles, pieces, pieces_other, row_count),
        [SMEM] + [VMEM] * 3 + [ANY],
        [struct((row_blocks, BLK + TAIL, BLK), BF16), struct((row_devices, BLK), F32)],
        [
            pltpu.VMEM((row_devices + 1, BLK, BLK), BF16),
            pltpu.VMEM((row_blocks, BLK, BLK), F32),
            pltpu.VMEM((row_blocks, BLK), F32),
            pltpu.VMEM((row_devices, BLK), F32),
            pltpu.SemaphoreType.DMA((2,)),
        ],
        work,
        out_specs=[VMEM, ANY],
    )
    message = lax.all_to_all(message, "col", 0, 0, tiled=True)
    width = weight.shape[1]
    chunk = BLK // row_blocks
    activations, message = call(
        node_kernel,
        "node",
        (message, weight, bias.reshape(1, width), out_cotangent),
        [VMEM] * 4,
        [
            struct((BLK, width), BF16),
            struct((row_blocks, BLK + 2 * chunk + TAIL, BLK), BF16),
        ],
        (),
        8 * BLK * BLK * width,
    )
    message = lax.all_to_all(message, "col", 0, 0, tiled=True)
    scratch = [pltpu.VMEM((row_blocks + 1, BLK, BLK), BF16), pltpu.VMEM((half, BLK, BLK), F32)]
    other = call(
        backward_other_kernel,
        "backward_other",
        (plan, tiles, message),
        [SMEM, VMEM, VMEM],
        struct((half * BLK + 4 * chunk + 16, BLK), BF16),
        scratch,
        work,
    )
    arrived = lax.ppermute(other, "row", partner)
    own = call(
        backward_own_kernel,
        "backward_own",
        (plan, tiles, message),
        [SMEM, VMEM, VMEM],
        struct((half, BLK, BLK), BF16),
        scratch,
        work,
    )
    message = call(
        pair_kernel,
        "pair",
        (message, own, arrived),
        [VMEM] * 3,
        struct((half, BLK + 2 * chunk + TAIL, BLK), BF16),
    )
    message = lax.all_to_all(message, "row", 0, 0, tiled=True, axis_index_groups=parities)
    chunks, grad_bias = call(
        tail_kernel,
        "tail",
        (message,),
        [VMEM],
        [struct((row_blocks, chunk, width), F32), struct((1, width), F32)],
    )
    grad_weight = lax.all_to_all(chunks, "col", 0, 0, tiled=True)
    grad_inputs = call(
        last_kernel, "last", (message, scale), [VMEM, VMEM], struct((BLK, BLK), BF16)
    )
    return activations, grad_inputs, grad_weight.reshape(BLK, width), grad_bias.reshape(width)


def solution(mesh):
    in_specs = (
        P(("col", "row"), None),
        P(),
        P(),
        P("row", "col", None, None),
        P("row", "col", None),
        P("row", "col"),
        P(("row", "col"), None),
    )
    out_specs = (P(("row", "col"), None), P(("col", "row"), None), P(), P())
    return jax.shard_map(
        per_device, mesh=mesh, in_specs=in_specs, out_specs=out_specs, check_vma=False
    )
```
